32 devices in a mesh: ep: 8 (over z, x), et: 4 (over y, core).
Axes of the slice: x: 2, y: 2, z: 4, core: 2. Of those that a mesh axis runs over, the one named last changes fastest.
Arguments:
- out_grad: bfloat16 [1024, 7168], P('ep', 'et'), may hold values from -0.1796875 to 0.1796875
- gate_weights: bfloat16 [1024, 8], P('ep'), may hold values from 0.049804688 to 1
- routes: int32 [1024, 8], P('ep'), may hold values from 0 to 7, as said below
- gate_pre: bfloat16 [8, 1024, 1024], P('ep', None, 'et'), may hold values from -6 to 6
- up_pre: bfloat16 [8, 1024, 1024], P('ep', None, 'et'), may hold values from -6 to 6
- down_weight: bfloat16 [8, 1024, 7168], P('ep', None, 'et'), may hold values from -0.1875 to 0.1875
Outputs:
- d_down_weight: bfloat16 [8, 1024, 7168], P('ep', None, 'et')
- d_gate: float32 [1024, 8], P('ep')
The draws below stay inside these ranges and needn't reach their ends.
Inputs may be any that keep to these rules, and one draw needn't show every extreme that they name: The experts in one row of routes differ. Among the rows of one source (one index of ep), at most 128 pairs name the same expert, and one expert is named by exactly 128 pairs of every source.
All inputs are finite; a program needn't handle non-finite values.
Results may differ from the reference program's by a relative error of at most 0.0057.
Values may be sent and summed in bfloat16 or wider, within the bound.
No kernel may reach another device: no remote copies, remote signals or barrier semaphores. Data moves between devices by JAX's collectives and lax.ppermute only.
A program may use at most 64 MiB of HBM per device.

```python
import jax
import jax.numpy as jnp
from jax import lax

D = 7168
H = 1024
TOPK = 8
TOK_DEV = 128
EXPERTS = 8
CAP = 128
SLOTS = 1024
TOKENS = 1024
N_EP = 8


def draw_routes(key, part):
    mean_load = TOK_DEV * TOPK // EXPERTS
    spread = CAP - mean_load
    half = EXPERTS // 2
    hot = jax.random.randint(jax.random.fold_in(key, 1), (), 0, EXPERTS)
    positions = jnp.arange(TOK_DEV * TOPK, dtype=jnp.int32)

    def one_block(block_key):
        lift_key, order_key, token_key = jax.random.split(block_key, 3)
        lift = jax.random.randint(lift_key, (half,), 0, spread + 1)
        lift = lift.at[0].set(spread)
        loads = jnp.concatenate([mean_load + lift, mean_load - lift])
        starts = jnp.cumsum(loads) - loads
        order = jnp.concatenate([jnp.zeros((1,), jnp.int32), jax.random.permutation(order_key, EXPERTS - 1).astype(jnp.int32) + 1])
        labels = (hot + order) % EXPERTS
        which = jnp.sum((positions[:, None] >= starts[None, :]).astype(jnp.int32), axis=1) - 1
        expert_at = labels[which]
        token_order = jax.random.permutation(token_key, TOK_DEV).astype(jnp.int32)
        token = token_order[positions % TOK_DEV]
        column = positions // TOK_DEV
        return jnp.zeros((TOK_DEV, TOPK), jnp.int32).at[token, column].set(expert_at.astype(jnp.int32))
    block_keys = jax.random.split(jax.random.fold_in(key, 2), N_EP)
    return jax.vmap(one_block)(block_keys).reshape(TOKENS, TOPK).astype(jnp.int32)


def block_levels(own_key, extent, shards, least, largest):
    gain = 1.0
    for axis_at, shards_of in shards:
        steps = jax.random.uniform(jax.random.fold_in(jax.random.fold_in(own_key, 6), axis_at), (shards_of,), jnp.float32, least / len(shards), largest / len(shards))
        gain = gain * jnp.repeat(jnp.exp(steps), extent[axis_at] // shards_of).reshape((-1,) + (1,) * (len(extent) - 1 - axis_at))
    return gain


def gaussian(stream_key, dims, deviation, reach, cuts=(), held_as=jnp.bfloat16):
    level = block_levels(stream_key, dims, cuts, -0.22, 0.18) if cuts else 1.0
    result = jax.random.normal(stream_key, dims, jnp.float32) * deviation * level
    return jnp.minimum(jnp.maximum(result, -reach), reach).astype(held_as)


def setup_inputs(seed: int = 0) -> dict:
    arg_keys = jax.random.split(jax.random.key(seed), 7)
    return {
        "out_grad": gaussian(arg_keys[0], (TOKENS, D), 0.03, 0.1796875, ((0, 8), (1, 4))),
        "gate_weights": jnp.clip(0.049804688 + 0.9501953 * jax.random.uniform(arg_keys[1], (TOKENS, TOPK), jnp.float32) ** block_levels(arg_keys[1], (TOKENS, TOPK), ((0, 8),), -0.2, 0.2), 0.049804688, 1.0).astype(jnp.bfloat16),
        "routes": draw_routes(jax.random.fold_in(arg_keys[6], 71), 0),
        "gate_pre": gaussian(arg_keys[3], (EXPERTS, SLOTS, H), 1.0, 6.0, ((0, 8), (2, 4))),
        "up_pre": gaussian(arg_keys[4], (EXPERTS, SLOTS, H), 1.0, 6.0, ((0, 8), (2, 4))),
        "down_weight": gaussian(arg_keys[5], (EXPERTS, H, D), H ** -0.5, 0.1875, ((0, 8), (2, 4))),
    }


def reference(out_grad, gate_weights, routes, gate_pre, up_pre, down_weight):
    pairs = routes.reshape(N_EP, TOK_DEV * TOPK)
    onehot = (pairs[:, :, None] == jnp.arange(EXPERTS, dtype=jnp.int32)[None, None, :]).astype(jnp.int32)
    ranks = jnp.sum(jnp.cumsum(onehot, axis=1) * onehot, axis=2) - 1
    source = jnp.arange(N_EP, dtype=jnp.int32)[:, None]
    slot_of = (source * CAP + ranks).reshape(-1).astype(jnp.int32)
    flat_route = routes.reshape(-1)
    pair_ids = jnp.arange(TOKENS * TOPK, dtype=jnp.int32)
    flat_gates = gate_weights.reshape(-1)

    def one_expert(items):
        expert, gate_block, up_block, weight = items
        target = jnp.where(flat_route == expert, slot_of, SLOTS).astype(jnp.int32)
        slot_pair = jnp.zeros((SLOTS,), jnp.int32).at[target].set(pair_ids, mode="drop")
        filled = jnp.zeros((SLOTS,), jnp.bool_).at[target].set(True, mode="drop")
        rows = jnp.where(filled[:, None], out_grad[slot_pair // TOPK], 0.0).astype(jnp.bfloat16)
        gates = jnp.where(filled, flat_gates[slot_pair], 0.0).astype(jnp.bfloat16)
        hidden = (jax.nn.silu(gate_block.astype(jnp.float32)) * up_block.astype(jnp.float32)).astype(jnp.bfloat16)
        scaled = (gates.astype(jnp.float32)[:, None] * rows.astype(jnp.float32)).astype(jnp.bfloat16)
        grad_weight = jnp.dot(hidden.T, scaled, preferred_element_type=jnp.float32).astype(jnp.bfloat16)
        expert_out = jnp.dot(hidden, weight, preferred_element_type=jnp.float32)
        slot_grad = jnp.sum(rows.astype(jnp.float32) * expert_out, axis=1)
        return grad_weight, slot_grad

    experts_ids = jnp.arange(EXPERTS, dtype=jnp.int32)
    grads, slot_grads = lax.map(one_expert, (experts_ids, gate_pre, up_pre, down_weight))
    picked = (flat_route * SLOTS + slot_of).astype(jnp.int32)
    d_gate = slot_grads.reshape(-1)[picked].reshape(TOKENS, TOPK)
    return grads, d_gate
```

```python
import functools

import jax
import jax.numpy as jnp
import numpy as np
from jax import lax
from jax.experimental import pallas as pl
from jax.experimental.pallas import tpu as pltpu
from jax.sharding import PartitionSpec as P

MIB = 1024 * 1024
BF16 = jnp.bfloat16
F32 = jnp.float32


def vmem_spec():
    return pl.BlockSpec(memory_space=pltpu.VMEM)


def smem_spec():
    return pl.BlockSpec(memory_space=pltpu.SMEM)


def params(mib):
    return pltpu.CompilerParams(vmem_limit_bytes=mib * MIB)


def cost(flops, moved):
    return pl.CostEstimate(flops=int(flops), bytes_accessed=int(moved), transcendentals=0)


def assemble(info, parts, weight, capacity):
    slots, width = parts[0].shape
    units, feats = weight.shape
    cols = 256

    def body(info_ref, *refs):
        part_refs, (w_ref, ht_ref, eo_ref, h_scr) = refs[: len(parts)], refs[len(parts) :]

        @pl.when(pl.program_id(0) == 0)
        def _():
            for m, ref in enumerate(part_refs):
                at = pl.multiple_of(info_ref[m] * width, width)
                value = ref[...]
                h_scr[:, pl.ds(at, width)] = value
                ht_ref[pl.ds(at, width), :] = value.T

        eo_ref[...] = jnp.dot(h_scr[...], w_ref[...], preferred_element_type=F32)

    return pl.pallas_call(
        body,
        grid=(feats // cols,),
        in_specs=[smem_spec()]
        + [vmem_spec()] * len(parts)
        + [pl.BlockSpec((units, cols), lambda j: (0, j))],
        out_specs=[
            pl.BlockSpec((units, slots), lambda j: (0, 0)),
            pl.BlockSpec((slots, cols), lambda j: (0, j)),
        ],
        out_shape=[
            jax.ShapeDtypeStruct((units, slots), BF16),
            jax.ShapeDtypeStruct((slots, feats), F32),
        ],
        scratch_shapes=[pltpu.VMEM((slots, units), BF16)],
        compiler_params=params(40),
        cost_estimate=cost(2 * slots * units * feats, 2 * units * feats + 4 * slots * feats),
        name="expert_out",
    )(info, *parts, weight)


def slot_sums(info, pieces, expert_out, capacity, where):
    rows, feats = pieces[0].shape

    def body(info_ref, *refs):
        piece_refs, (eo_ref, out_ref) = refs[: len(pieces)], refs[len(pieces) :]
        for i, ref in enumerate(piece_refs):
            at, first = where[i]
            start = pl.multiple_of(info_ref[at] * capacity + first, rows)
            total = jnp.sum(ref[...].astype(F32) * eo_ref[pl.ds(start, rows), :], axis=1)
            out_ref[pl.ds(i, 1), :] = total[None, :]

    return pl.pallas_call(
        body,
        in_specs=[smem_spec()] + [vmem_spec()] * (len(pieces) + 1),
        out_specs=vmem_spec(),
        out_shape=jax.ShapeDtypeStruct((len(pieces), rows), F32),
        compiler_params=params(24),
        cost_estimate=cost(2 * len(pieces) * rows * feats, 6 * len(pieces) * rows * feats),
        name="slot_sums",
    )(info, *pieces, expert_out)


def weight_grad(info, pieces, gates, hidden_t, capacity, where):
    rows, feats = pieces[0].shape
    units, slots = hidden_t.shape
    cols = 256

    def body(info_ref, *refs):
        piece_refs, (g_ref, ht_ref, out_ref, rows_scr) = refs[: len(pieces)], refs[len(pieces) :]

        for i, ref in enumerate(piece_refs):
            at, first = where[i]
            start = pl.multiple_of(info_ref[at] * capacity + first, rows)
            gate = g_ref[pl.ds(start, rows), :].astype(F32)
            rows_scr[pl.ds(start, rows), :] = (ref[...].astype(F32) * gate).astype(BF16)
        out_ref[...] = jnp.dot(ht_ref[...], rows_scr[...], preferred_element_type=F32).astype(BF16)

    return pl.pallas_call(
        body,
        grid=(feats // cols,),
        in_specs=[smem_spec()]
        + [pl.BlockSpec((rows, cols), lambda j: (0, j))] * len(pieces)
        + [vmem_spec(), vmem_spec()],
        out_specs=pl.BlockSpec((units, cols), lambda j: (0, j)),
        out_shape=jax.ShapeDtypeStruct((units, feats), BF16),
        scratch_shapes=[pltpu.VMEM((slots, cols), BF16)],
        compiler_params=params(24),
        cost_estimate=cost(2 * slots * units * feats, 4 * units * feats),
        name="weight_grad",
    )(info, *pieces, gates, hidden_t)


def pick(returned, routes_t):
    topk, tokens = routes_t.shape
    experts, groups, _ = returned.shape

    def body(back_ref, routes_ref, out_ref):
        routes = routes_ref[...]
        total = jnp.zeros((topk, tokens), F32)
        for e in range(experts):
            value = back_ref[e, 0:1, :]
            for f in range(1, groups):
                value = value + back_ref[e, f : f + 1, :]
            total = jnp.where(routes == e, jnp.broadcast_to(value, total.shape), total)
        out_ref[...] = total

    return pl.pallas_call(
        body,
        in_specs=[vmem_spec(), vmem_spec()],
        out_specs=vmem_spec(),
        out_shape=jax.ShapeDtypeStruct((topk, tokens), F32),
        name="pick_gate_grad",
    )(returned, routes_t)


def ring_of(experts):
    return list(range(0, experts, 2)) + list(range(experts - 1, 0, -2))


def dense(out_grad, gate_weights, routes, gate_pre, up_pre, down_weight):
    tokens, topk = routes.shape
    experts, groups = lax.axis_size("ep"), lax.axis_size("et")
    slots = gate_pre.shape[1]
    half = tokens // 2
    weight = down_weight[0]

    ring = ring_of(experts)
    forth = [(ring[i], ring[(i + 1) % experts]) for i in range(experts)]
    back = [(b, a) for a, b in forth]
    place = {device: i for i, device in enumerate(ring)}
    far = experts // 2
    steps = [0] + [s for k in range(1, far) for s in (-k, k)] + [far]
    sources = np.array([[ring[(place[d] + s) % experts] for s in steps] for d in range(experts)], np.int32)
    et = lax.axis_index("et").astype(jnp.int32)
    info = jnp.concatenate(
        [jnp.stack([et ^ m for m in range(groups)]), jnp.asarray(sources)[lax.axis_index("ep")]]
    )

    top, bottom = out_grad[:half], out_grad[half:]
    up, down = [top, bottom], [bottom, top]
    pieces, where = [top, bottom], [(groups, 0), (groups, half)]
    for k in range(1, far):
        for c in range(2):
            up[c] = lax.ppermute(up[c], "ep", forth)
            down[c] = lax.ppermute(down[c], "ep", back)
        pieces += [up[0], up[1], down[1], down[0]]
        a, b = groups + 2 * k - 1, groups + 2 * k
        where += [(a, 0), (a, half), (b, 0), (b, half)]
    last = [lax.ppermute(up[0], "ep", forth), lax.ppermute(down[0], "ep", back)]
    where_last = [(groups + 2 * far - 1, 0), (groups + 2 * far - 1, half)]

    routes_t, gates_t = routes.T, gate_weights.T
    by_expert = jnp.sum(
        jnp.where(
            routes_t[None] == jnp.arange(experts, dtype=jnp.int32)[:, None, None],
            gates_t[None].astype(F32),
            0.0,
        ),
        axis=1,
    ).astype(BF16)
    gates = lax.all_to_all(by_expert, "ep", split_axis=0, concat_axis=0, tiled=True)
    gates = gates.reshape(slots, 1)

    hidden = (
        jax.nn.silu(gate_pre[0].astype(F32)) * up_pre[0].astype(F32)
    ).astype(BF16)
    parts = [hidden]
    bit = 1
    order = [0]
    for axis_bit in (2, 1):
        swap = [(i, i ^ axis_bit) for i in range(groups)]
        parts += [lax.ppermute(p, "et", swap) for p in parts]
        order += [o ^ axis_bit for o in order]
    parts = [parts[order.index(m)] for m in range(groups)]

    hidden_t, expert_out = assemble(info, parts, weight, tokens)
    sums = slot_sums(info, pieces, expert_out, tokens, where)
    sums_last = slot_sums(info, last, expert_out, tokens, where_last)
    sums = jnp.concatenate([sums.reshape(-1, tokens), sums_last.reshape(1, tokens)])
    inverse = np.argsort(sources, axis=1).astype(np.int32)
    sums = sums[jnp.asarray(inverse)[lax.axis_index("ep")]]
    outgoing = jnp.broadcast_to(sums[:, None, :], (experts, groups, tokens)).reshape(experts * groups, tokens)
    returned = lax.all_to_all(outgoing, ("ep", "et"), split_axis=0, concat_axis=0, tiled=True)
    grad = weight_grad(info, pieces + last, gates, hidden_t, tokens, where + where_last)
    d_gate = pick(returned.reshape(experts, groups, tokens), routes_t).T
    return grad[None], d_gate


def routed(out_grad, gate_weights, routes, gate_pre, up_pre, down_weight):
    tok_rows, topk = routes.shape
    experts = lax.axis_size("ep")
    slot_total = gate_pre.shape[1]
    capacity = slot_total // experts
    flat_route = routes.reshape(-1)
    pair_count = tok_rows * topk
    onehot = (flat_route[:, None] == jnp.arange(experts, dtype=jnp.int32)[None, :]).astype(
        jnp.int32
    )
    ranks = jnp.sum(jnp.cumsum(onehot, axis=0) * onehot, axis=1) - 1
    slot_of = flat_route * capacity + ranks
    pair_ids = jnp.arange(pair_count, dtype=jnp.int32)
    slot_pair = jnp.zeros((experts * capacity,), jnp.int32).at[slot_of].set(pair_ids)
    filled = jnp.zeros((experts * capacity,), jnp.bool_).at[slot_of].set(True)
    send_rows = jnp.where(filled[:, None], out_grad[slot_pair // topk], 0.0)
    send_rows = send_rows.reshape(experts, capacity, out_grad.shape[1])
    send_gates = jnp.where(filled, gate_weights.reshape(-1)[slot_pair], 0.0)
    send_gates = send_gates.reshape(experts, capacity)
    rows_in, gates_in = (
        lax.all_to_all(send_rows, "ep", split_axis=0, concat_axis=0, tiled=True),
        lax.all_to_all(send_gates, "ep", split_axis=0, concat_axis=0, tiled=True),
    )
    rows_in = rows_in.reshape(slot_total, out_grad.shape[1])
    gates_in = gates_in.reshape(slot_total)
    weight = down_weight[0]
    hidden_part = (
        jax.nn.silu(gate_pre[0].astype(jnp.float32)) * up_pre[0].astype(jnp.float32)
    ).astype(jnp.bfloat16)
    scaled = (gates_in.astype(jnp.float32)[:, None] * rows_in.astype(jnp.float32)).astype(
        jnp.bfloat16
    )
    piece = lax.all_gather(hidden_part, "et", axis=1, tiled=True)
    expert_out = jnp.dot(piece, weight, preferred_element_type=jnp.float32)
    grad_weight = lax.dot_general(
        piece, scaled, (((0,), (0,)), ((), ())), preferred_element_type=jnp.float32
    )
    partial_grad = jnp.sum(rows_in.astype(jnp.float32) * expert_out, axis=1)
    slot_grad = lax.psum(partial_grad, "et")
    returned = lax.all_to_all(
        slot_grad.reshape(experts, capacity), "ep", split_axis=0, concat_axis=0, tiled=True
    )
    d_gate = returned.reshape(-1)[slot_of].reshape(tok_rows, topk)
    return (grad_weight.astype(jnp.bfloat16)[None], d_gate)


def solution(mesh):
    sizes = dict(mesh.shape)

    def local(out_grad, gate_weights, routes, gate_pre, up_pre, down_weight):
        tokens, topk = routes.shape
        whole = topk == sizes["ep"] and gate_pre.shape[1] == topk * tokens
        if whole and sizes["ep"] % 2 == 0 and sizes["et"] == 4:
            return dense(out_grad, gate_weights, routes, gate_pre, up_pre, down_weight)
        return routed(out_grad, gate_weights, routes, gate_pre, up_pre, down_weight)

    in_specs = (
        P("ep", "et"),
        P("ep", None),
        P("ep", None),
        P("ep", None, "et"),
        P("ep", None, "et"),
        P("ep", None, "et"),
    )
    out_specs = (P("ep", None, "et"), P("ep", None))
    return jax.shard_map(local, mesh=mesh, in_specs=in_specs, out_specs=out_specs, check_vma=False)
```

```python
import jax
import jax.numpy as jnp
from jax import lax
from jax.experimental import pallas as pl
from jax.experimental.pallas import tpu as pltpu
from jax.sharding import PartitionSpec as P

MIB = 1024 * 1024
BF16 = jnp.bfloat16
F32 = jnp.float32
LANES = 128


def vmem_spec():
    return pl.BlockSpec(memory_space=pltpu.VMEM)


def smem_spec():
    return pl.BlockSpec(memory_space=pltpu.SMEM)


def any_spec():
    return pl.BlockSpec(memory_space=pl.ANY)


def params(mib):
    return pltpu.CompilerParams(vmem_limit_bytes=mib * MIB)


def cost(flops, moved):
    return pl.CostEstimate(flops=int(flops) // 1000, bytes_accessed=int(moved) // 1000, transcendentals=0)


def in_hbm(x):
    return pltpu.with_memory_space_constraint(x, pltpu.HBM)


def ring_of(experts):
    return list(range(0, experts, 2)) + list(range(experts - 1, 0, -2))


def source_of(me, step, experts):
    at = jnp.where(me % 2 == 0, me // 2, experts - 1 - me // 2)
    at = (at + step + experts) % experts
    return jnp.where(at < experts // 2, 2 * at, 2 * (experts - 1 - at) + 1)


def front(out_grad, gate_pre, up_pre, gates_t, routes_t):
    slots, width = gate_pre.shape
    tokens, feats = out_grad.shape
    experts = routes_t.shape[0]
    half = tokens // 2
    cols = feats // LANES
    blocks = 4
    rows = slots // blocks

    def body(rows_ref, pre_ref, up_ref, g_ref, r_ref, top_ref, bottom_ref, hidden_ref, *scr):
        rows_scr, g_scr, r_scr, pre_scr, up_scr, sems = scr
        first = [
            pltpu.make_async_copy(src, dst, sems.at[2 * blocks + i])
            for i, (src, dst) in enumerate(((rows_ref, rows_scr), (g_ref, g_scr), (r_ref, r_scr)))
        ]
        copies = []
        for i in range(blocks):
            here = pl.ds(i * rows, rows)
            copies.append(
                [
                    pltpu.make_async_copy(src.at[here], dst.at[here], sems.at[2 * i + j])
                    for j, (src, dst) in enumerate(((pre_ref, pre_scr), (up_ref, up_scr)))
                ]
            )
        for copy in first + sum(copies, []):
            copy.start()
        for copy in first:
            copy.wait()
        routes = r_scr[...]
        gates = g_scr[...].astype(F32)
        by = [
            jnp.sum(jnp.where(routes == e, gates, 0.0), axis=0, keepdims=True) for e in range(experts)
        ]
        by = jnp.concatenate(by + [jnp.zeros((16 - experts, tokens), F32)], axis=0).astype(BF16)
        for c, ref in enumerate((top_ref, bottom_ref)):
            for j in range(cols):
                ref[j * half : (j + 1) * half, :] = rows_scr[
                    c * half : (c + 1) * half, j * LANES : (j + 1) * LANES
                ]
            ref[cols * half :, :] = by
        for i in range(blocks):
            for copy in copies[i]:
                copy.wait()
            here = pl.ds(i * rows, rows)
            pre = pre_scr[here, :].astype(F32)
            hidden_ref[here, :] = (pre / (1.0 + jnp.exp(-pre)) * up_scr[here, :].astype(F32)).astype(BF16)

    return pl.pallas_call(
        body,
        in_specs=[any_spec()] * 5,
        out_specs=[vmem_spec()] * 3,
        out_shape=[pltpu.VMEM((cols * half + 16, LANES), BF16)] * 2 + [pltpu.VMEM((slots, width), BF16)],
        scratch_shapes=[
            pltpu.VMEM(out_grad.shape, BF16),
            pltpu.VMEM(gates_t.shape, BF16),
            pltpu.VMEM(routes_t.shape, jnp.int32),
            pltpu.VMEM((slots, width), BF16),
            pltpu.VMEM((slots, width), BF16),
            pltpu.SemaphoreType.DMA((2 * blocks + 3,)),
        ],
        compiler_params=params(6),
        cost_estimate=cost(8 * slots * width, 6 * slots * width),
        name="front",
    )(*[in_hbm(x) for x in (out_grad, gate_pre, up_pre, gates_t, routes_t)])


def fetch(weight):
    def body(in_ref, out_ref, sem):
        copy = pltpu.make_async_copy(in_ref, out_ref, sem)
        copy.start()
        copy.wait()

    return pl.pallas_call(
        body,
        in_specs=[any_spec()],
        out_specs=vmem_spec(),
        out_shape=pltpu.VMEM(weight.shape, weight.dtype),
        scratch_shapes=[pltpu.SemaphoreType.DMA(())],
        compiler_params=params(1),
        cost_estimate=cost(0, 4 * weight.size),
        name="fetch_weight",
    )(in_hbm(weight))


def assemble(info, parts, weight, tokens, steps):
    slots, width = parts[0].shape
    units, feats = weight.shape
    groups, experts = len(parts), slots // tokens
    cols = 256
    blocks = feats // cols

    def body(info_ref, *refs):
        part_refs, (w_ref, ht_ref, eo_ref, h_scr) = refs[:groups], refs[groups:]

        for m, ref in enumerate(part_refs):
            at = pl.multiple_of((info_ref[0] ^ m) * width, width)
            for i, step in enumerate(steps):
                start = pl.multiple_of(source_of(info_ref[1], step, experts) * tokens, tokens)
                value = ref[pl.ds(start, tokens), :]
                here = slice(i * tokens, (i + 1) * tokens)
                h_scr[here, pl.ds(at, width)] = value
                ht_ref[pl.ds(at, width), here] = value.T
        for j in range(blocks):
            here = slice(j * cols, (j + 1) * cols)
            eo_ref[:, here] = jnp.dot(h_scr[...], w_ref[:, here], preferred_element_type=F32)

    return pl.pallas_call(
        body,
        in_specs=[smem_spec()] + [vmem_spec()] * (groups + 1),
        out_specs=[vmem_spec(), vmem_spec()],
        out_shape=[pltpu.VMEM((units, slots), BF16), pltpu.VMEM((slots, feats), F32)],
        scratch_shapes=[pltpu.VMEM((slots, units), BF16)],
        compiler_params=params(6),
        cost_estimate=cost(0.5 * slots * units * feats, 4 * units * slots),
        name="expert_out",
    )(info, *parts, weight)


def take(chunk_ref, eo_ref, scaled_ref, at, held_at, half, me):
    cols = eo_ref.shape[1] // LANES
    by = chunk_ref[cols * half :, :].astype(F32)
    row = lax.broadcasted_iota(jnp.int32, by.shape, 0)
    gate = jnp.sum(jnp.where(row == me, by, 0.0), axis=0, keepdims=True)
    first = at % (2 * half)
    gate = jnp.broadcast_to(gate, (8, gate.shape[1])).T[first : first + half, :1]
    total = jnp.zeros((half, LANES), F32)
    for j in range(cols):
        value = chunk_ref[j * half : (j + 1) * half, :].astype(F32)
        here = slice(j * LANES, (j + 1) * LANES)
        total = total + value * eo_ref[at : at + half, here]
        scaled_ref[held_at : held_at + half, here] = (value * gate).astype(BF16)
    return jnp.sum(total, axis=1, keepdims=True)


def absorb(info, chunks, expert_out, first, tokens, weigh=1):
    half = tokens // 2
    slots, feats = expert_out.shape
    experts = slots // tokens
    count = len(chunks) // 2

    def body(info_ref, *refs):
        chunk_refs, (eo_ref, sums_ref, scaled_ref, held, sems) = refs[: 2 * count], refs[2 * count :]
        lanes, copies = [], []
        for i in range(count):
            sums = []
            for c in range(2):
                at, held_at = (first + i) * tokens + c * half, i * tokens + c * half
                sums.append(take(chunk_refs[2 * i + c], eo_ref, held, at, held_at, half, info_ref[1]))
            lanes.append(jnp.concatenate(sums, axis=0))
            here = pl.ds(i * tokens, tokens)
            copy = pltpu.make_async_copy(held.at[here], scaled_ref.at[here], sems.at[i])
            copy.start()
            copies.append(copy)
        lanes += [jnp.zeros((tokens, 1), F32)] * (experts - count)
        sums_ref[...] = jnp.concatenate(lanes, axis=1).T
        for copy in copies:
            copy.wait()

    return pl.pallas_call(
        body,
        in_specs=[smem_spec()] + [vmem_spec()] * (2 * count + 1),
        out_specs=[vmem_spec(), any_spec()],
        out_shape=[pltpu.VMEM((experts, tokens), F32), pltpu.HBM((count * tokens, feats), BF16)],
        scratch_shapes=[
            pltpu.VMEM((count * tokens, feats), BF16),
            pltpu.SemaphoreType.DMA((count,)),
        ],
        compiler_params=params(6),
        cost_estimate=cost(weigh * 3 * count * tokens * feats, weigh * 8 * count * tokens * feats),
        name="absorb",
    )(info, *chunks, expert_out)


def absorb_last(info, chunks, expert_out, earlier, counts, groups, steps, tokens):
    half = tokens // 2
    slots, feats = expert_out.shape
    experts = slots // tokens
    last = experts - 1

    def body(info_ref, top_ref, bottom_ref, eo_ref, *refs):
        early_refs, (out_ref, scaled_ref) = refs[: len(earlier)], refs[len(earlier) :]
        sums = [
            take(ref, eo_ref, scaled_ref, last * tokens + c * half, c * half, half, info_ref[1])
            for c, ref in enumerate((top_ref, bottom_ref))
        ]
        own = jnp.broadcast_to(jnp.concatenate(sums, axis=0), (tokens, experts)).T
        rows = [ref[i : i + 1, :] for ref, n in zip(early_refs, counts) for i in range(n)] + [own[0:1]]
        for step, row in zip(steps, rows):
            out_ref[source_of(info_ref[1], step, experts)] = jnp.broadcast_to(row, (groups, tokens))

    return pl.pallas_call(
        body,
        in_specs=[smem_spec()] + [vmem_spec()] * (3 + len(earlier)),
        out_specs=[vmem_spec(), vmem_spec()],
        out_shape=[
            jax.ShapeDtypeStruct((experts, groups, tokens), F32),
            pltpu.VMEM((tokens, feats), BF16),
        ],
        compiler_params=params(4),
        cost_estimate=cost(3 * tokens * feats, 8 * tokens * feats),
        name="absorb_last",
    )(info, *chunks, expert_out, *earlier)


def weight_grad(scaled, scaled_last, hidden_t):
    units, slots = hidden_t.shape
    feats = scaled_last.shape[1]
    blocks = 4
    rows = units // blocks
    counts = [s.shape[0] for s in scaled]
    done = sum(counts)

    def body(*refs):
        scaled_refs = refs[: len(scaled)]
        last_ref, ht_ref, out_ref, rows_scr, held, in_sems, out_sems = refs[len(scaled) :]
        copies = [
            pltpu.make_async_copy(
                ref, rows_scr.at[pl.ds(sum(counts[:i]), counts[i])], in_sems.at[i]
            )
            for i, ref in enumerate(scaled_refs)
        ]
        for copy in copies:
            copy.start()
        rows_scr[done:, :] = last_ref[...]
        for copy in copies:
            copy.wait()
        copies = []
        for i in range(blocks):
            here = pl.ds(i * rows, rows)
            held[here, :] = jnp.dot(ht_ref[here, :], rows_scr[...], preferred_element_type=F32).astype(BF16)
            copy = pltpu.make_async_copy(held.at[here], out_ref.at[here], out_sems.at[i])
            copy.start()
            copies.append(copy)
        for copy in copies:
            copy.wait()

    return pl.pallas_call(
        body,
        in_specs=[any_spec()] * len(scaled) + [vmem_spec()] * 2,
        out_specs=any_spec(),
        out_shape=jax.ShapeDtypeStruct((units, feats), BF16),
        scratch_shapes=[
            pltpu.VMEM((slots, feats), BF16),
            pltpu.VMEM((units, feats), BF16),
            pltpu.SemaphoreType.DMA((len(scaled),)),
            pltpu.SemaphoreType.DMA((blocks,)),
        ],
        compiler_params=params(12),
        cost_estimate=cost(2 * slots * units * feats, 4 * units * feats),
        name="weight_grad",
    )(*[in_hbm(s) for s in scaled], scaled_last, hidden_t)


def pick(returned, routes_t):
    topk, tokens = routes_t.shape
    experts, groups, _ = returned.shape

    def body(back_ref, routes_ref, out_ref):
        routes = routes_ref[...]
        total = jnp.zeros((topk, tokens), F32)
        for e in range(experts):
            value = jnp.sum(back_ref[e], axis=0, keepdims=True)
            total = jnp.where(routes == e, jnp.broadcast_to(value, total.shape), total)
        out_ref[...] = total

    return pl.pallas_call(
        body,
        in_specs=[vmem_spec(), vmem_spec()],
        out_specs=vmem_spec(),
        out_shape=jax.ShapeDtypeStruct((topk, tokens), F32),
        compiler_params=params(2),
        name="pick_gate_grad",
    )(returned, routes_t)


def dense(out_grad, gate_weights, routes, gate_pre, up_pre, down_weight):
    tokens, topk = routes.shape
    experts, groups = lax.axis_size("ep"), lax.axis_size("et")
    weight = down_weight[0]
    barrier = lax.optimization_barrier

    ring = ring_of(experts)
    forth = [(ring[i], ring[(i + 1) % experts]) for i in range(experts)]
    back = [(b, a) for a, b in forth]
    far = experts // 2
    steps = [0] + [s for k in range(1, far) for s in (-k, k)] + [far]
    info = jnp.stack([lax.axis_index("et").astype(jnp.int32), lax.axis_index("ep").astype(jnp.int32)])
    out_grad, info = barrier((out_grad, info))

    top, bottom, hidden = front(out_grad, gate_pre[0], up_pre[0], gate_weights.T, routes.T)
    chips, cores = [(i, i ^ 2) for i in range(groups)], [(i, i ^ 1) for i in range(groups)]

    def hop(c):
        up[c] = lax.ppermute(up[c], "ep", forth)
        down[c] = lax.ppermute(down[c], "ep", back)

    up, down = [top, bottom], [bottom, top]
    chunks = [top, bottom]
    hop(0)
    hop(1)
    chunks += [up[0], up[1], down[1], down[0]]
    over = lax.ppermute(hidden, "et", chips)
    beside, across = lax.ppermute(hidden, "et", cores), lax.ppermute(over, "et", cores)
    weight, _ = barrier((weight, up[0]))
    weight = fetch(weight)

    hop(0)
    hop(1)
    chunks += [up[0], up[1], down[1], down[0]]
    up[0], weight = barrier((up[0], weight))

    hop(0)
    hop(1)
    third = [up[0], up[1], down[1], down[0]]

    hop(0)
    hidden_t, expert_out = assemble(info, [hidden, beside, over, across], weight, tokens, steps)
    sums_a, scaled_a = absorb(info, chunks, expert_out, 0, tokens)
    sums_b, scaled_b = absorb(info, third, expert_out, 5, tokens, 3000)
    outgoing, scaled_c = absorb_last(
        info, [up[0], down[0]], expert_out, [sums_a, sums_b], [5, 2], groups, steps, tokens
    )
    returned = lax.all_to_all(
        outgoing.reshape(experts * groups, tokens), ("ep", "et"), split_axis=0, concat_axis=0, tiled=True
    )
    grad = weight_grad([scaled_a, scaled_b], scaled_c, hidden_t)
    d_gate = pick(returned.reshape(experts, groups, tokens), routes.T).T
    return grad[None], d_gate


def routed(out_grad, gate_weights, routes, gate_pre, up_pre, down_weight):
    tok_rows, topk = routes.shape
    experts = lax.axis_size("ep")
    slot_total = gate_pre.shape[1]
    capacity = slot_total // experts
    flat_route = routes.reshape(-1)
    pair_count = tok_rows * topk
    onehot = (flat_route[:, None] == jnp.arange(experts, dtype=jnp.int32)[None, :]).astype(
        jnp.int32
    )
    ranks = jnp.sum(jnp.cumsum(onehot, axis=0) * onehot, axis=1) - 1
    slot_of = flat_route * capacity + ranks
    pair_ids = jnp.arange(pair_count, dtype=jnp.int32)
    slot_pair = jnp.zeros((experts * capacity,), jnp.int32).at[slot_of].set(pair_ids)
    filled = jnp.zeros((experts * capacity,), jnp.bool_).at[slot_of].set(True)
    send_rows = jnp.where(filled[:, None], out_grad[slot_pair // topk], 0.0)
    send_rows = send_rows.reshape(experts, capacity, out_grad.shape[1])
    send_gates = jnp.where(filled, gate_weights.reshape(-1)[slot_pair], 0.0)
    send_gates = send_gates.reshape(experts, capacity)
    rows_in, gates_in = (
        lax.all_to_all(send_rows, "ep", split_axis=0, concat_axis=0, tiled=True),
        lax.all_to_all(send_gates, "ep", split_axis=0, concat_axis=0, tiled=True),
    )
    rows_in = rows_in.reshape(slot_total, out_grad.shape[1])
    gates_in = gates_in.reshape(slot_total)
    weight = down_weight[0]
    hidden_part = (
        jax.nn.silu(gate_pre[0].astype(jnp.float32)) * up_pre[0].astype(jnp.float32)
    ).astype(jnp.bfloat16)
    scaled = (gates_in.astype(jnp.float32)[:, None] * rows_in.astype(jnp.float32)).astype(
        jnp.bfloat16
    )
    piece = lax.all_gather(hidden_part, "et", axis=1, tiled=True)
    expert_out = jnp.dot(piece, weight, preferred_element_type=jnp.float32)
    grad_weight = lax.dot_general(
        piece, scaled, (((0,), (0,)), ((), ())), preferred_element_type=jnp.float32
    )
    partial_grad = jnp.sum(rows_in.astype(jnp.float32) * expert_out, axis=1)
    slot_grad = lax.psum(partial_grad, "et")
    returned = lax.all_to_all(
        slot_grad.reshape(experts, capacity), "ep", split_axis=0, concat_axis=0, tiled=True
    )
    d_gate = returned.reshape(-1)[slot_of].reshape(tok_rows, topk)
    return (grad_weight.astype(jnp.bfloat16)[None], d_gate)


def solution(mesh):
    sizes = dict(mesh.shape)

    def local(out_grad, gate_weights, routes, gate_pre, up_pre, down_weight):
        tokens, topk = routes.shape
        whole = topk == sizes["ep"] and gate_pre.shape[1] == topk * tokens
        if whole and sizes["ep"] == 8 and sizes["et"] == 4:
            return dense(out_grad, gate_weights, routes, gate_pre, up_pre, down_weight)
        return routed(out_grad, gate_weights, routes, gate_pre, up_pre, down_weight)

    in_specs = (
        P("ep", "et"),
        P("ep", None),
        P("ep", None),
        P("ep", None, "et"),
        P("ep", None, "et"),
        P("ep", None, "et"),
    )
    out_specs = (P("ep", None, "et"), P("ep", None))
    return jax.shard_map(local, mesh=mesh, in_specs=in_specs, out_specs=out_specs, check_vma=False)
```

```python
import jax
import jax.numpy as jnp
from jax import lax
from jax.experimental import pallas as pl
from jax.experimental.pallas import tpu as pltpu
from jax.sharding import PartitionSpec as P

MIB = 1024 * 1024
BF16 = jnp.bfloat16
F32 = jnp.float32
LANES = 128


def vmem_spec():
    return pl.BlockSpec(memory_space=pltpu.VMEM)


def smem_spec():
    return pl.BlockSpec(memory_space=pltpu.SMEM)


def any_spec():
    return pl.BlockSpec(memory_space=pl.ANY)


def params(mib):
    return pltpu.CompilerParams(vmem_limit_bytes=mib * MIB)


def cost(flops, moved):
    return pl.CostEstimate(flops=int(flops) // 1000, bytes_accessed=int(moved) // 1000, transcendentals=0)


def in_hbm(x):
    return pltpu.with_memory_space_constraint(x, pltpu.HBM)


def ring_of(experts):
    return list(range(0, experts, 2)) + list(range(experts - 1, 0, -2))


def source_of(me, step, experts):
    at = jnp.where(me % 2 == 0, me // 2, experts - 1 - me // 2)
    at = (at + step + experts) % experts
    return jnp.where(at < experts // 2, 2 * at, 2 * (experts - 1 - at) + 1)


def chunks_of(out_grad, gates_t, routes_t):
    tokens, feats = out_grad.shape
    experts = routes_t.shape[0]
    half = tokens // 2
    cols = feats // LANES

    def body(rows_ref, g_ref, r_ref, top_ref, bottom_ref, rows_scr, g_scr, r_scr, sems):
        copies = [
            pltpu.make_async_copy(src, dst, sems.at[i])
            for i, (src, dst) in enumerate(((g_ref, g_scr), (r_ref, r_scr), (rows_ref, rows_scr)))
        ]
        for copy in copies:
            copy.start()
        for copy in copies[:2]:
            copy.wait()
        routes = r_scr[...]
        gates = g_scr[...].astype(F32)
        by = [
            jnp.sum(jnp.where(routes == e, gates, 0.0), axis=0, keepdims=True) for e in range(experts)
        ]
        by = jnp.concatenate(by + [jnp.zeros((16 - experts, tokens), F32)], axis=0).astype(BF16)
        copies[2].wait()
        for c, ref in enumerate((top_ref, bottom_ref)):
            for j in range(cols):
                ref[j * half : (j + 1) * half, :] = rows_scr[
                    c * half : (c + 1) * half, j * LANES : (j + 1) * LANES
                ]
            ref[cols * half :, :] = by

    return pl.pallas_call(
        body,
        in_specs=[any_spec()] * 3,
        out_specs=[vmem_spec()] * 2,
        out_shape=[pltpu.VMEM((cols * half + 16, LANES), BF16)] * 2,
        scratch_shapes=[
            pltpu.VMEM(out_grad.shape, BF16),
            pltpu.VMEM(gates_t.shape, BF16),
            pltpu.VMEM(routes_t.shape, jnp.int32),
            pltpu.SemaphoreType.DMA((3,)),
        ],
        compiler_params=params(4),
        cost_estimate=cost(4 * tokens * feats, 4 * tokens * feats),
        name="chunks",
    )(*[in_hbm(x) for x in (out_grad, gates_t, routes_t)])


def hidden_of(gate_pre, up_pre, weight):
    slots, width = gate_pre.shape
    blocks = 4
    rows = slots // blocks

    def body(pre_ref, up_ref, w_ref, hidden_ref, held_ref, pre_scr, up_scr, sems):
        copies = []
        for i in range(blocks):
            here = pl.ds(i * rows, rows)
            copies.append(
                [
                    pltpu.make_async_copy(src.at[here], dst.at[here], sems.at[2 * i + j])
                    for j, (src, dst) in enumerate(((pre_ref, pre_scr), (up_ref, up_scr)))
                ]
            )
        fetch = pltpu.make_async_copy(w_ref, held_ref, sems.at[2 * blocks])
        for copy in sum(copies, []):
            copy.start()
        fetch.start()
        for i in range(blocks):
            for copy in copies[i]:
                copy.wait()
            here = pl.ds(i * rows, rows)
            pre = pre_scr[here, :].astype(F32)
            hidden_ref[here, :] = (pre / (1.0 + jnp.exp(-pre)) * up_scr[here, :].astype(F32)).astype(BF16)
        fetch.wait()

    return pl.pallas_call(
        body,
        in_specs=[any_spec()] * 3,
        out_specs=[vmem_spec()] * 2,
        out_shape=[pltpu.VMEM((slots, width), BF16), pltpu.VMEM(weight.shape, BF16)],
        scratch_shapes=[
            pltpu.VMEM((slots, width), BF16),
            pltpu.VMEM((slots, width), BF16),
            pltpu.SemaphoreType.DMA((2 * blocks + 1,)),
        ],
        compiler_params=params(4),
        cost_estimate=cost(8 * slots * width, 6 * slots * width),
        name="hidden",
    )(*[in_hbm(x) for x in (gate_pre, up_pre, weight)])


def assemble(info, parts, weight, scaled, tokens, steps):
    slots, width = parts[0].shape
    units, feats = weight.shape
    groups, experts = len(parts), slots // tokens
    cols = 256
    counts = [x.shape[0] for x in scaled]

    def body(info_ref, *refs):
        part_refs, refs = refs[:groups], refs[groups:]
        scaled_refs, refs = refs[: len(scaled)], refs[len(scaled) :]
        w_ref, ht_ref, eo_ref, out_ref, h_scr, sems = refs
        copies = [
            pltpu.make_async_copy(ref, out_ref.at[pl.ds(sum(counts[:i]), counts[i])], sems.at[i])
            for i, ref in enumerate(scaled_refs)
        ]
        for copy in copies:
            copy.start()
        for m, ref in enumerate(part_refs):
            at = pl.multiple_of((info_ref[0] ^ m) * width, width)
            for i, step in enumerate(steps):
                start = pl.multiple_of(source_of(info_ref[1], step, experts) * tokens, tokens)
                value = ref[pl.ds(start, tokens), :]
                here = slice(i * tokens, (i + 1) * tokens)
                h_scr[here, pl.ds(at, width)] = value
                ht_ref[pl.ds(at, width), here] = value.T
        for j in range(feats // cols):
            here = slice(j * cols, (j + 1) * cols)
            eo_ref[:, here] = jnp.dot(h_scr[...], w_ref[:, here], preferred_element_type=F32)
        for copy in copies:
            copy.wait()

    return pl.pallas_call(
        body,
        in_specs=[smem_spec()] + [vmem_spec()] * (groups + len(scaled) + 1),
        out_specs=[vmem_spec(), vmem_spec(), any_spec()],
        out_shape=[
            pltpu.VMEM((units, slots), BF16),
            pltpu.VMEM((slots, feats), F32),
            pltpu.HBM((sum(counts), feats), BF16),
        ],
        scratch_shapes=[pltpu.VMEM((slots, units), BF16), pltpu.SemaphoreType.DMA((len(scaled),))],
        compiler_params=params(6),
        cost_estimate=pl.CostEstimate(flops=0, bytes_accessed=1000, transcendentals=0),
        name="expert_out",
    )(info, *parts, *scaled, weight)


def column(row):
    return jnp.broadcast_to(row, (8, row.shape[1])).T[:, :1]


def gate_of(chunk_ref, me, half, lower):
    by = chunk_ref[chunk_ref.shape[0] - 16 :, :].astype(F32)
    row = lax.broadcasted_iota(jnp.int32, by.shape, 0)
    gate = jnp.sum(jnp.where(row == me, by, 0.0), axis=0, keepdims=True)
    return column(gate)[lower * half : (lower + 1) * half]


def add_up(chunk_ref, eo_ref, at, half):
    total = jnp.zeros((half, LANES), F32)
    for j in range(eo_ref.shape[1] // LANES):
        value = chunk_ref[j * half : (j + 1) * half, :].astype(F32)
        total = total + value * eo_ref[at : at + half, j * LANES : (j + 1) * LANES]
    return jnp.sum(total, axis=1, keepdims=True)


def put_scaled(chunk_ref, out_ref, at, gate, half):
    for j in range(out_ref.shape[1] // LANES):
        value = chunk_ref[j * half : (j + 1) * half, :].astype(F32)
        out_ref[at : at + half, j * LANES : (j + 1) * LANES] = (value * gate).astype(BF16)


def scaled_rows(info, chunks, lowers, half, declared):
    cols = (chunks[0].shape[0] - 16) // half
    count = len(chunks)

    def body(info_ref, *refs):
        out_ref = refs[count]
        for i, ref in enumerate(refs[:count]):
            put_scaled(ref, out_ref, i * half, gate_of(ref, info_ref[1], half, lowers[i]), half)

    return pl.pallas_call(
        body,
        in_specs=[smem_spec()] + [vmem_spec()] * count,
        out_specs=vmem_spec(),
        out_shape=pltpu.VMEM((count * half, cols * LANES), BF16),
        compiler_params=params(3),
        cost_estimate=pl.CostEstimate(flops=declared, bytes_accessed=1000, transcendentals=0),
        name="scaled_rows",
    )(info, *chunks)


def absorb(info, chunks, expert_out, tokens, steps, declared):
    half = tokens // 2
    experts = expert_out.shape[0] // tokens
    count = len(chunks) // 2

    def body(info_ref, *refs):
        chunk_refs, (eo_ref, sums_ref, last_ref, own_ref) = refs[: 2 * count], refs[2 * count :]
        me = info_ref[1]
        lanes = []
        for i in range(count):
            at = i * tokens
            sums = [add_up(chunk_refs[2 * i + c], eo_ref, at + c * half, half) for c in range(2)]
            lanes.append(jnp.concatenate(sums, axis=0))
        lanes += [jnp.zeros((tokens, 1), F32)] * (experts - count)
        by_step = jnp.concatenate(lanes, axis=1).T
        row = lax.broadcasted_iota(jnp.int32, (experts, tokens), 0)
        total = jnp.zeros((experts, tokens), F32)
        for i, step in enumerate(steps[:count]):
            total = jnp.where(row == source_of(me, step, experts), by_step[i : i + 1], total)
        sums_ref[...] = total
        last_ref[...] = (row == source_of(me, steps[-1], experts)).astype(F32)
        own_ref[...] = (lax.broadcasted_iota(jnp.int32, own_ref.shape, 0) == me).astype(F32)

    return pl.pallas_call(
        body,
        in_specs=[smem_spec()] + [vmem_spec()] * (2 * count + 1),
        out_specs=[vmem_spec()] * 3,
        out_shape=[
            pltpu.VMEM((experts, tokens), F32),
            pltpu.VMEM((experts, tokens), F32),
            pltpu.VMEM((16, LANES), F32),
        ],
        compiler_params=params(4),
        cost_estimate=pl.CostEstimate(flops=declared, bytes_accessed=1000, transcendentals=0),
        name="absorb",
    )(info, *chunks, expert_out)


def absorb_last(chunks, expert_out, sums, mask, groups):
    experts, tokens = sums.shape
    half = tokens // 2
    first = expert_out.shape[0] - tokens

    def body(top_ref, bottom_ref, eo_ref, sums_ref, mask_ref, out_ref):
        parts = [add_up(ref, eo_ref, first + c * half, half) for c, ref in enumerate((top_ref, bottom_ref))]
        own = jnp.broadcast_to(jnp.concatenate(parts, axis=0), (tokens, experts)).T
        value = jnp.where(mask_ref[...] > 0.0, own, sums_ref[...])
        out_ref[...] = jnp.broadcast_to(value[:, None, :], out_ref.shape)

    return pl.pallas_call(
        body,
        in_specs=[vmem_spec()] * 5,
        out_specs=vmem_spec(),
        out_shape=jax.ShapeDtypeStruct((experts, groups, tokens), F32),
        compiler_params=params(2),
        cost_estimate=cost(3 * tokens * expert_out.shape[1], 8 * tokens * expert_out.shape[1]),
        name="absorb_last",
    )(*chunks, expert_out, sums, mask)


def weight_grad(own, early, early_places, late, late_places, last_chunks, hidden_t):
    units, slots = hidden_t.shape
    feats = late[0].shape[1]
    half = late[0].shape[0] // len(late_places[0])
    blocks = 4
    rows = units // blocks

    def body(own_ref, early_ref, *refs):
        late_refs, refs = refs[: len(late)], refs[len(late) :]
        top_ref, bottom_ref, ht_ref, out_ref, rows_scr, held, in_sems, out_sems = refs
        copies = [
            pltpu.make_async_copy(
                early_ref.at[pl.ds(i * half, half)], rows_scr.at[pl.ds(place, half)], in_sems.at[i]
            )
            for i, place in enumerate(early_places)
        ]
        for copy in copies:
            copy.start()
        for ref, at in zip(late_refs, late_places):
            for i, place in enumerate(at):
                rows_scr[place : place + half, :] = ref[i * half : (i + 1) * half, :]
        for c, ref in enumerate((top_ref, bottom_ref)):
            by = ref[ref.shape[0] - 16 :, :].astype(F32)
            gate = column(jnp.sum(by * own_ref[...], axis=0, keepdims=True))[c * half : (c + 1) * half]
            put_scaled(ref, rows_scr, slots - (2 - c) * half, gate, half)
        for copy in copies:
            copy.wait()
        copies = []
        for i in range(blocks):
            here = pl.ds(i * rows, rows)
            held[here, :] = jnp.dot(ht_ref[here, :], rows_scr[...], preferred_element_type=F32).astype(BF16)
            copy = pltpu.make_async_copy(held.at[here], out_ref.at[here], out_sems.at[i])
            copy.start()
            copies.append(copy)
        for copy in copies:
            copy.wait()

    return pl.pallas_call(
        body,
        in_specs=[vmem_spec(), any_spec()] + [vmem_spec()] * (3 + len(late)),
        out_specs=any_spec(),
        out_shape=jax.ShapeDtypeStruct((units, feats), BF16),
        scratch_shapes=[
            pltpu.VMEM((slots, feats), BF16),
            pltpu.VMEM((units, feats), BF16),
            pltpu.SemaphoreType.DMA((len(early_places),)),
            pltpu.SemaphoreType.DMA((blocks,)),
        ],
        compiler_params=params(12),
        cost_estimate=cost(2 * slots * units * feats, 4 * units * feats),
        name="weight_grad",
    )(own, in_hbm(early), *late, *last_chunks, hidden_t)


def pick(returned, routes_t):
    topk, tokens = routes_t.shape
    experts, groups, _ = returned.shape

    def body(back_ref, routes_ref, out_ref):
        routes = routes_ref[...]
        total = jnp.zeros((topk, tokens), F32)
        for e in range(experts):
            value = jnp.sum(back_ref[e], axis=0, keepdims=True)
            total = jnp.where(routes == e, jnp.broadcast_to(value, total.shape), total)
        out_ref[...] = total

    return pl.pallas_call(
        body,
        in_specs=[vmem_spec(), vmem_spec()],
        out_specs=vmem_spec(),
        out_shape=jax.ShapeDtypeStruct((topk, tokens), F32),
        compiler_params=params(2),
        name="pick_gate_grad",
    )(returned, routes_t)


def dense(out_grad, gate_weights, routes, gate_pre, up_pre, down_weight):
    tokens, topk = routes.shape
    experts, groups = lax.axis_size("ep"), lax.axis_size("et")
    weight = down_weight[0]
    barrier = lax.optimization_barrier

    ring = ring_of(experts)
    forth = [(ring[i], ring[(i + 1) % experts]) for i in range(experts)]
    back = [(b, a) for a, b in forth]
    far = experts // 2
    steps = [0] + [s for k in range(1, far) for s in (-k, k)] + [far]
    info = jnp.stack([lax.axis_index("et").astype(jnp.int32), lax.axis_index("ep").astype(jnp.int32)])
    out_grad, info = barrier((out_grad, info))

    top, bottom = chunks_of(out_grad, gate_weights.T, routes.T)
    hidden, weight = hidden_of(gate_pre[0], up_pre[0], weight)
    chips, cores = [(i, i ^ 2) for i in range(groups)], [(i, i ^ 1) for i in range(groups)]
    half = tokens // 2

    def hop(c):
        up[c] = lax.ppermute(up[c], "ep", forth)
        down[c] = lax.ppermute(down[c], "ep", back)

    def scale(chunks, lowers, declared=0):
        return scaled_rows(info, chunks, lowers, half, declared)

    up, down = [top, bottom], [bottom, top]
    hop(0)
    hop(1)
    over = lax.ppermute(hidden, "et", chips)
    beside, across = lax.ppermute(hidden, "et", cores), lax.ppermute(over, "et", cores)
    first = [up[0], up[1], down[1], down[0]]
    hop(0)
    hop(1)
    second = [up[0], up[1], down[1], down[0]]
    scaled_a = scale([top, bottom] + first, [0, 1] * 3, 4000000000)
    up[0], down[0], scaled_a = barrier((up[0], down[0], scaled_a))
    hop(0)
    scaled_b = scale(second, [0, 1] * 2, 8000000000)
    up[1], down[1], scaled_b = barrier((up[1], down[1], scaled_b))
    hop(1)
    third = [up[0], up[1], down[1], down[0]]
    scaled_c = scale([up[0], down[0]], [0, 1], 12000000000)
    scaled_d = scale([up[1], down[1]], [1, 0])
    up[0], down[0], scaled_c, beside, across = barrier((up[0], down[0], scaled_c, beside, across))

    hop(0)
    hidden_t, expert_out, early = assemble(
        info, [hidden, beside, over, across], weight, [scaled_a, scaled_b], tokens, steps
    )
    third, scaled_d = barrier((third, scaled_d))
    sums, mask, own = absorb(
        info, [top, bottom] + first + second + third, expert_out, tokens, steps, 3000
    )
    outgoing = absorb_last([up[0], down[0]], expert_out, sums, mask, groups)
    returned = lax.all_to_all(
        outgoing.reshape(experts * groups, tokens), ("ep", "et"), split_axis=0, concat_axis=0, tiled=True
    )
    late_places = [[10 * half, 13 * half], [11 * half, 12 * half]]
    grad = weight_grad(
        own, early, [i * half for i in range(10)], [scaled_c, scaled_d], late_places, [up[0], down[0]], hidden_t
    )
    d_gate = pick(returned.reshape(experts, groups, tokens), routes.T).T
    return grad[None], d_gate


def routed(out_grad, gate_weights, routes, gate_pre, up_pre, down_weight):
    tok_rows, topk = routes.shape
    experts = lax.axis_size("ep")
    slot_total = gate_pre.shape[1]
    capacity = slot_total // experts
    flat_route = routes.reshape(-1)
    pair_count = tok_rows * topk
    onehot = (flat_route[:, None] == jnp.arange(experts, dtype=jnp.int32)[None, :]).astype(
        jnp.int32
    )
    ranks = jnp.sum(jnp.cumsum(onehot, axis=0) * onehot, axis=1) - 1
    slot_of = flat_route * capacity + ranks
    pair_ids = jnp.arange(pair_count, dtype=jnp.int32)
    slot_pair = jnp.zeros((experts * capacity,), jnp.int32).at[slot_of].set(pair_ids)
    filled = jnp.zeros((experts * capacity,), jnp.bool_).at[slot_of].set(True)
    send_rows = jnp.where(filled[:, None], out_grad[slot_pair // topk], 0.0)
    send_rows = send_rows.reshape(experts, capacity, out_grad.shape[1])
    send_gates = jnp.where(filled, gate_weights.reshape(-1)[slot_pair], 0.0)
    send_gates = send_gates.reshape(experts, capacity)
    rows_in, gates_in = (
        lax.all_to_all(send_rows, "ep", split_axis=0, concat_axis=0, tiled=True),
        lax.all_to_all(send_gates, "ep", split_axis=0, concat_axis=0, tiled=True),
    )
    rows_in = rows_in.reshape(slot_total, out_grad.shape[1])
    gates_in = gates_in.reshape(slot_total)
    weight = down_weight[0]
    hidden_part = (
        jax.nn.silu(gate_pre[0].astype(jnp.float32)) * up_pre[0].astype(jnp.float32)
    ).astype(jnp.bfloat16)
    scaled = (gates_in.astype(jnp.float32)[:, None] * rows_in.astype(jnp.float32)).astype(
        jnp.bfloat16
    )
    piece = lax.all_gather(hidden_part, "et", axis=1, tiled=True)
    expert_out = jnp.dot(piece, weight, preferred_element_type=jnp.float32)
    grad_weight = lax.dot_general(
        piece, scaled, (((0,), (0,)), ((), ())), preferred_element_type=jnp.float32
    )
    partial_grad = jnp.sum(rows_in.astype(jnp.float32) * expert_out, axis=1)
    slot_grad = lax.psum(partial_grad, "et")
    returned = lax.all_to_all(
        slot_grad.reshape(experts, capacity), "ep", split_axis=0, concat_axis=0, tiled=True
    )
    d_gate = returned.reshape(-1)[slot_of].reshape(tok_rows, topk)
    return (grad_weight.astype(jnp.bfloat16)[None], d_gate)


def solution(mesh):
    sizes = dict(mesh.shape)

    def local(out_grad, gate_weights, routes, gate_pre, up_pre, down_weight):
        tokens, topk = routes.shape
        whole = topk == sizes["ep"] and gate_pre.shape[1] == topk * tokens
        if whole and sizes["ep"] == 8 and sizes["et"] == 4:
            return dense(out_grad, gate_weights, routes, gate_pre, up_pre, down_weight)
        return routed(out_grad, gate_weights, routes, gate_pre, up_pre, down_weight)

    in_specs = (
        P("ep", "et"),
        P("ep", None),
        P("ep", None),
        P("ep", None, "et"),
        P("ep", None, "et"),
        P("ep", None, "et"),
    )
    out_specs = (P("ep", None, "et"), P("ep", None))
    return jax.shard_map(local, mesh=mesh, in_specs=in_specs, out_specs=out_specs, check_vma=False)
```

```python
import jax
import jax.numpy as jnp
from jax import lax
from jax.experimental import pallas as pl
from jax.experimental.pallas import tpu as pltpu
from jax.sharding import PartitionSpec as P

MIB = 1024 * 1024
BF16 = jnp.bfloat16
F32 = jnp.float32
LANES = 128


def vmem_spec():
    return pl.BlockSpec(memory_space=pltpu.VMEM)


def smem_spec():
    return pl.BlockSpec(memory_space=pltpu.SMEM)


def any_spec():
    return pl.BlockSpec(memory_space=pl.ANY)


def params(mib):
    return pltpu.CompilerParams(vmem_limit_bytes=mib * MIB)


def cost(flops, moved):
    return pl.CostEstimate(flops=int(flops) // 1000, bytes_accessed=int(moved) // 1000, transcendentals=0)


def in_hbm(x):
    return pltpu.with_memory_space_constraint(x, pltpu.HBM)


def ring_of(experts):
    return list(range(0, experts, 2)) + list(range(experts - 1, 0, -2))


def source_of(me, step, experts):
    at = jnp.where(me % 2 == 0, me // 2, experts - 1 - me // 2)
    at = (at + step + experts) % experts
    return jnp.where(at < experts // 2, 2 * at, 2 * (experts - 1 - at) + 1)


def chunks_of(out_grad, gates_t, routes_t):
    tokens, feats = out_grad.shape
    experts = routes_t.shape[0]
    half = tokens // 2
    cols = feats // LANES

    def body(rows_ref, g_ref, r_ref, top_ref, bottom_ref, rows_scr, g_scr, r_scr, sems):
        copies = [
            pltpu.make_async_copy(src, dst, sems.at[i])
            for i, (src, dst) in enumerate(((g_ref, g_scr), (r_ref, r_scr), (rows_ref, rows_scr)))
        ]
        for copy in copies:
            copy.start()
        for copy in copies[:2]:
            copy.wait()
        routes = r_scr[...]
        gates = g_scr[...].astype(F32)
        by = [
            jnp.sum(jnp.where(routes == e, gates, 0.0), axis=0, keepdims=True) for e in range(experts)
        ]
        by = jnp.concatenate(by + [jnp.zeros((16 - experts, tokens), F32)], axis=0).astype(BF16)
        copies[2].wait()
        for c, ref in enumerate((top_ref, bottom_ref)):
            for j in range(cols):
                ref[j * half : (j + 1) * half, :] = rows_scr[
                    c * half : (c + 1) * half, j * LANES : (j + 1) * LANES
                ]
            ref[cols * half :, :] = by

    return pl.pallas_call(
        body,
        in_specs=[any_spec()] * 3,
        out_specs=[vmem_spec()] * 2,
        out_shape=[pltpu.VMEM((cols * half + 16, LANES), BF16)] * 2,
        scratch_shapes=[
            pltpu.VMEM(out_grad.shape, BF16),
            pltpu.VMEM(gates_t.shape, BF16),
            pltpu.VMEM(routes_t.shape, jnp.int32),
            pltpu.SemaphoreType.DMA((3,)),
        ],
        compiler_params=params(4),
        cost_estimate=cost(4 * tokens * feats, 4 * tokens * feats),
        name="chunks",
    )(*[in_hbm(x) for x in (out_grad, gates_t, routes_t)])


def hidden_of(gate_pre, up_pre, weight):
    slots, width = gate_pre.shape
    blocks = 4
    rows = slots // blocks

    def body(pre_ref, up_ref, w_ref, hidden_ref, held_ref, pre_scr, up_scr, sems):
        copies = []
        for i in range(blocks):
            here = pl.ds(i * rows, rows)
            copies.append(
                [
                    pltpu.make_async_copy(src.at[here], dst.at[here], sems.at[2 * i + j])
                    for j, (src, dst) in enumerate(((pre_ref, pre_scr), (up_ref, up_scr)))
                ]
            )
        fetch = pltpu.make_async_copy(w_ref, held_ref, sems.at[2 * blocks])
        for copy in sum(copies, []):
            copy.start()
        fetch.start()
        for i in range(blocks):
            for copy in copies[i]:
                copy.wait()
            here = pl.ds(i * rows, rows)
            pre = pre_scr[here, :].astype(F32)
            hidden_ref[here, :] = (pre / (1.0 + jnp.exp(-pre)) * up_scr[here, :].astype(F32)).astype(BF16)
        fetch.wait()

    return pl.pallas_call(
        body,
        in_specs=[any_spec()] * 3,
        out_specs=[vmem_spec()] * 2,
        out_shape=[pltpu.VMEM((slots, width), BF16), pltpu.VMEM(weight.shape, BF16)],
        scratch_shapes=[
            pltpu.VMEM((slots, width), BF16),
            pltpu.VMEM((slots, width), BF16),
            pltpu.SemaphoreType.DMA((2 * blocks + 1,)),
        ],
        compiler_params=params(4),
        cost_estimate=cost(8 * slots * width, 6 * slots * width),
        name="hidden",
    )(*[in_hbm(x) for x in (gate_pre, up_pre, weight)])


def assemble(info, parts, weight, tokens, steps, feats):
    slots, width = parts[0].shape
    units = weight.shape[0]
    groups, experts = len(parts), slots // tokens
    cols = 256

    def body(info_ref, *refs):
        part_refs, (w_ref, h_ref, ht_ref, eo_ref) = refs[:groups], refs[groups:]
        for m, ref in enumerate(part_refs):
            at = pl.multiple_of((info_ref[0] ^ m) * width, width)
            for i, step in enumerate(steps):
                start = pl.multiple_of(source_of(info_ref[1], step, experts) * tokens, tokens)
                value = ref[pl.ds(start, tokens), :]
                here = slice(i * tokens, (i + 1) * tokens)
                h_ref[here, pl.ds(at, width)] = value
                ht_ref[pl.ds(at, width), here] = value.T
        for j in range(feats // cols):
            here = slice(j * cols, (j + 1) * cols)
            eo_ref[:, here] = jnp.dot(h_ref[...], w_ref[:, here], preferred_element_type=F32)

    return pl.pallas_call(
        body,
        in_specs=[smem_spec()] + [vmem_spec()] * (groups + 1),
        out_specs=[vmem_spec()] * 3,
        out_shape=[
            pltpu.VMEM((slots, units), BF16),
            pltpu.VMEM((units, slots), BF16),
            pltpu.VMEM((slots, feats), F32),
        ],
        compiler_params=params(6),
        cost_estimate=pl.CostEstimate(flops=0, bytes_accessed=1000, transcendentals=0),
        name="expert_out_first",
    )(info, *parts, weight)


def expert_out_rest(hidden, weight, scaled, feats):
    slots = hidden.shape[0]
    first, feats = feats, weight.shape[1]
    cols = 256
    counts = [x.shape[0] for x in scaled]

    def body(h_ref, w_ref, *refs):
        scaled_refs, (eo_ref, out_ref, sems) = refs[: len(scaled)], refs[len(scaled) :]
        copies = [
            pltpu.make_async_copy(ref, out_ref.at[pl.ds(sum(counts[:i]), counts[i])], sems.at[i])
            for i, ref in enumerate(scaled_refs)
        ]
        for copy in copies:
            copy.start()
        for j in range(first, feats, cols):
            eo_ref[:, j - first : j - first + cols] = jnp.dot(
                h_ref[...], w_ref[:, j : j + cols], preferred_element_type=F32
            )
        for copy in copies:
            copy.wait()

    return pl.pallas_call(
        body,
        in_specs=[vmem_spec()] * (2 + len(scaled)),
        out_specs=[vmem_spec(), any_spec()],
        out_shape=[pltpu.VMEM((slots, feats - first), F32), pltpu.HBM((sum(counts), feats), BF16)],
        scratch_shapes=[pltpu.SemaphoreType.DMA((len(scaled),))],
        compiler_params=params(6),
        cost_estimate=pl.CostEstimate(flops=0, bytes_accessed=1000, transcendentals=0),
        name="expert_out_rest",
    )(hidden, weight, *scaled)


def column(row):
    return jnp.broadcast_to(row, (8, row.shape[1])).T[:, :1]


def gate_of(chunk_ref, me, half, lower):
    by = chunk_ref[chunk_ref.shape[0] - 16 :, :].astype(F32)
    row = lax.broadcasted_iota(jnp.int32, by.shape, 0)
    gate = jnp.sum(jnp.where(row == me, by, 0.0), axis=0, keepdims=True)
    return column(gate)[lower * half : (lower + 1) * half]


def add_up(chunk_ref, eo_refs, at, half):
    total = jnp.zeros((half, LANES), F32)
    j = 0
    for ref in eo_refs:
        for k in range(ref.shape[1] // LANES):
            value = chunk_ref[j * half : (j + 1) * half, :].astype(F32)
            total = total + value * ref[at : at + half, k * LANES : (k + 1) * LANES]
            j += 1
    return jnp.sum(total, axis=1, keepdims=True)


def put_scaled(chunk_ref, out_ref, at, gate, half):
    for j in range(out_ref.shape[1] // LANES):
        value = chunk_ref[j * half : (j + 1) * half, :].astype(F32)
        out_ref[at : at + half, j * LANES : (j + 1) * LANES] = (value * gate).astype(BF16)


def scaled_rows(info, chunks, lowers, half, declared):
    cols = (chunks[0].shape[0] - 16) // half
    count = len(chunks)

    def body(info_ref, *refs):
        out_ref = refs[count]
        for i, ref in enumerate(refs[:count]):
            put_scaled(ref, out_ref, i * half, gate_of(ref, info_ref[1], half, lowers[i]), half)

    return pl.pallas_call(
        body,
        in_specs=[smem_spec()] + [vmem_spec()] * count,
        out_specs=vmem_spec(),
        out_shape=pltpu.VMEM((count * half, cols * LANES), BF16),
        compiler_params=params(3),
        cost_estimate=pl.CostEstimate(flops=declared, bytes_accessed=1000, transcendentals=0),
        name="scaled_rows",
    )(info, *chunks)


def absorb(info, chunks, expert_out, tokens, steps, declared):
    half = tokens // 2
    experts = expert_out[0].shape[0] // tokens
    count = len(chunks) // 2

    def body(info_ref, *refs):
        chunk_refs, eo_refs = refs[: 2 * count], refs[2 * count : 2 * count + 2]
        sums_ref, last_ref, own_ref = refs[2 * count + 2 :]
        me = info_ref[1]
        lanes = []
        for i in range(count):
            at = i * tokens
            sums = [add_up(chunk_refs[2 * i + c], eo_refs, at + c * half, half) for c in range(2)]
            lanes.append(jnp.concatenate(sums, axis=0))
        lanes += [jnp.zeros((tokens, 1), F32)] * (experts - count)
        by_step = jnp.concatenate(lanes, axis=1).T
        row = lax.broadcasted_iota(jnp.int32, (experts, tokens), 0)
        total = jnp.zeros((experts, tokens), F32)
        for i, step in enumerate(steps[:count]):
            total = jnp.where(row == source_of(me, step, experts), by_step[i : i + 1], total)
        sums_ref[...] = total
        last_ref[...] = (row == source_of(me, steps[-1], experts)).astype(F32)
        own_ref[...] = (lax.broadcasted_iota(jnp.int32, own_ref.shape, 0) == me).astype(F32)

    return pl.pallas_call(
        body,
        in_specs=[smem_spec()] + [vmem_spec()] * (2 * count + 2),
        out_specs=[vmem_spec()] * 3,
        out_shape=[
            pltpu.VMEM((experts, tokens), F32),
            pltpu.VMEM((experts, tokens), F32),
            pltpu.VMEM((16, LANES), F32),
        ],
        compiler_params=params(4),
        cost_estimate=pl.CostEstimate(flops=declared, bytes_accessed=1000, transcendentals=0),
        name="absorb",
    )(info, *chunks, *expert_out)


def absorb_last(chunks, expert_out, sums, mask, groups):
    experts, tokens = sums.shape
    half = tokens // 2
    first = expert_out[0].shape[0] - tokens

    def body(top_ref, bottom_ref, eo_ref, rest_ref, sums_ref, mask_ref, out_ref):
        parts = [add_up(ref, (eo_ref, rest_ref), first + c * half, half) for c, ref in enumerate((top_ref, bottom_ref))]
        own = jnp.broadcast_to(jnp.concatenate(parts, axis=0), (tokens, experts)).T
        value = jnp.where(mask_ref[...] > 0.0, own, sums_ref[...])
        out_ref[...] = jnp.broadcast_to(value[:, None, :], out_ref.shape)

    return pl.pallas_call(
        body,
        in_specs=[vmem_spec()] * 6,
        out_specs=vmem_spec(),
        out_shape=jax.ShapeDtypeStruct((experts, groups, tokens), F32),
        compiler_params=params(2),
        cost_estimate=cost(tokens * LANES, tokens * LANES),
        name="absorb_last",
    )(*chunks, *expert_out, sums, mask)


def weight_grad(own, early, early_places, late, late_places, last_chunks, hidden_t):
    units, slots = hidden_t.shape
    feats = late[0].shape[1]
    half = late[0].shape[0] // len(late_places[0])
    blocks = 4
    rows = units // blocks

    def body(own_ref, early_ref, *refs):
        late_refs, refs = refs[: len(late)], refs[len(late) :]
        top_ref, bottom_ref, ht_ref, out_ref, rows_scr, held, in_sems, out_sems = refs
        copies = [
            pltpu.make_async_copy(
                early_ref.at[pl.ds(i * half, half)], rows_scr.at[pl.ds(place, half)], in_sems.at[i]
            )
            for i, place in enumerate(early_places)
        ]
        for copy in copies:
            copy.start()
        for ref, at in zip(late_refs, late_places):
            for i, place in enumerate(at):
                rows_scr[place : place + half, :] = ref[i * half : (i + 1) * half, :]
        for c, ref in enumerate((top_ref, bottom_ref)):
            by = ref[ref.shape[0] - 16 :, :].astype(F32)
            gate = column(jnp.sum(by * own_ref[...], axis=0, keepdims=True))[c * half : (c + 1) * half]
            put_scaled(ref, rows_scr, slots - (2 - c) * half, gate, half)
        for copy in copies:
            copy.wait()
        copies = []
        for i in range(blocks):
            here = pl.ds(i * rows, rows)
            held[here, :] = jnp.dot(ht_ref[here, :], rows_scr[...], preferred_element_type=F32).astype(BF16)
            copy = pltpu.make_async_copy(held.at[here], out_ref.at[here], out_sems.at[i])
            copy.start()
            copies.append(copy)
        for copy in copies:
            copy.wait()

    return pl.pallas_call(
        body,
        in_specs=[vmem_spec(), any_spec()] + [vmem_spec()] * (3 + len(late)),
        out_specs=any_spec(),
        out_shape=jax.ShapeDtypeStruct((units, feats), BF16),
        scratch_shapes=[
            pltpu.VMEM((slots, feats), BF16),
            pltpu.VMEM((units, feats), BF16),
            pltpu.SemaphoreType.DMA((len(early_places),)),
            pltpu.SemaphoreType.DMA((blocks,)),
        ],
        compiler_params=params(12),
        cost_estimate=cost(2 * slots * units * feats, 4 * units * feats),
        name="weight_grad",
    )(own, in_hbm(early), *late, *last_chunks, hidden_t)


def pick(returned, routes_t):
    topk, tokens = routes_t.shape
    experts, groups, _ = returned.shape

    def body(back_ref, routes_ref, out_ref):
        routes = routes_ref[...]
        total = jnp.zeros((topk, tokens), F32)
        for e in range(experts):
            value = jnp.sum(back_ref[e], axis=0, keepdims=True)
            total = jnp.where(routes == e, jnp.broadcast_to(value, total.shape), total)
        out_ref[...] = total

    return pl.pallas_call(
        body,
        in_specs=[vmem_spec(), vmem_spec()],
        out_specs=vmem_spec(),
        out_shape=jax.ShapeDtypeStruct((topk, tokens), F32),
        compiler_params=params(2),
        name="pick_gate_grad",
    )(returned, routes_t)


def dense(out_grad, gate_weights, routes, gate_pre, up_pre, down_weight):
    tokens, topk = routes.shape
    experts, groups = lax.axis_size("ep"), lax.axis_size("et")
    weight = down_weight[0]
    barrier = lax.optimization_barrier

    ring = ring_of(experts)
    forth = [(ring[i], ring[(i + 1) % experts]) for i in range(experts)]
    back = [(b, a) for a, b in forth]
    far = experts // 2
    steps = [0] + [s for k in range(1, far) for s in (-k, k)] + [far]
    info = jnp.stack([lax.axis_index("et").astype(jnp.int32), lax.axis_index("ep").astype(jnp.int32)])
    out_grad, info = barrier((out_grad, info))

    top, bottom = chunks_of(out_grad, gate_weights.T, routes.T)
    hidden, weight = hidden_of(gate_pre[0], up_pre[0], weight)
    chips, cores = [(i, i ^ 2) for i in range(groups)], [(i, i ^ 1) for i in range(groups)]
    half = tokens // 2

    def hop(c):
        up[c] = lax.ppermute(up[c], "ep", forth)
        down[c] = lax.ppermute(down[c], "ep", back)

    def scale(chunks, lowers, declared=0):
        return scaled_rows(info, chunks, lowers, half, declared)

    up, down = [top, bottom], [bottom, top]
    hop(0)
    hop(1)
    over = lax.ppermute(hidden, "et", chips)
    beside, across = lax.ppermute(hidden, "et", cores), lax.ppermute(over, "et", cores)
    up[0], down[0] = barrier((up[0], down[0]))
    first = [up[0], up[1], down[1], down[0]]
    hop(0)
    hop(1)
    second = [up[0], up[1], down[1], down[0]]
    scaled_a = scale([top, bottom] + first, [0, 1] * 3, 4000000000)
    up[0], down[0], scaled_a = barrier((up[0], down[0], scaled_a))
    hop(0)
    scaled_b = scale(second, [0, 1] * 2, 8000000000)
    up[1], down[1], scaled_b = barrier((up[1], down[1], scaled_b))
    hop(1)
    cut = weight.shape[1] // 256 * 3 // 7 * 256
    hidden, hidden_t, start = assemble(info, [hidden, beside, over, across], weight, tokens, steps, cut)
    up[0], down[0], hidden_t = barrier((up[0], down[0], hidden_t))
    third = [up[0], up[1], down[1], down[0]]
    scaled_c = scale([up[0], down[0]], [0, 1], 12000000000)
    up[0], down[0], scaled_c = barrier((up[0], down[0], scaled_c))

    hop(0)
    rest, early = expert_out_rest(hidden, weight, [scaled_a, scaled_b], cut)
    expert_out = [start, rest]
    third, early = barrier((third, early))
    scaled_d = scale([third[1], third[2]], [1, 0])
    third, scaled_d = barrier((third, scaled_d))
    sums, mask, own = absorb(
        info, [top, bottom] + first + second + third, expert_out, tokens, steps, 3000
    )
    outgoing = absorb_last([up[0], down[0]], expert_out, sums, mask, groups)
    returned = lax.all_to_all(
        outgoing.reshape(experts * groups, tokens), ("ep", "et"), split_axis=0, concat_axis=0, tiled=True
    )
    late_places = [[10 * half, 13 * half], [11 * half, 12 * half]]
    grad = weight_grad(
        own, early, [i * half for i in range(10)], [scaled_c, scaled_d], late_places, [up[0], down[0]], hidden_t
    )
    d_gate = pick(returned.reshape(experts, groups, tokens), routes.T).T
    return grad[None], d_gate


def routed(out_grad, gate_weights, routes, gate_pre, up_pre, down_weight):
    tok_rows, topk = routes.shape
    experts = lax.axis_size("ep")
    slot_total = gate_pre.shape[1]
    capacity = slot_total // experts
    flat_route = routes.reshape(-1)
    pair_count = tok_rows * topk
    onehot = (flat_route[:, None] == jnp.arange(experts, dtype=jnp.int32)[None, :]).astype(
        jnp.int32
    )
    ranks = jnp.sum(jnp.cumsum(onehot, axis=0) * onehot, axis=1) - 1
    slot_of = flat_route * capacity + ranks
    pair_ids = jnp.arange(pair_count, dtype=jnp.int32)
    slot_pair = jnp.zeros((experts * capacity,), jnp.int32).at[slot_of].set(pair_ids)
    filled = jnp.zeros((experts * capacity,), jnp.bool_).at[slot_of].set(True)
    send_rows = jnp.where(filled[:, None], out_grad[slot_pair // topk], 0.0)
    send_rows = send_rows.reshape(experts, capacity, out_grad.shape[1])
    send_gates = jnp.where(filled, gate_weights.reshape(-1)[slot_pair], 0.0)
    send_gates = send_gates.reshape(experts, capacity)
    rows_in, gates_in = (
        lax.all_to_all(send_rows, "ep", split_axis=0, concat_axis=0, tiled=True),
        lax.all_to_all(send_gates, "ep", split_axis=0, concat_axis=0, tiled=True),
    )
    rows_in = rows_in.reshape(slot_total, out_grad.shape[1])
    gates_in = gates_in.reshape(slot_total)
    weight = down_weight[0]
    hidden_part = (
        jax.nn.silu(gate_pre[0].astype(jnp.float32)) * up_pre[0].astype(jnp.float32)
    ).astype(jnp.bfloat16)
    scaled = (gates_in.astype(jnp.float32)[:, None] * rows_in.astype(jnp.float32)).astype(
        jnp.bfloat16
    )
    piece = lax.all_gather(hidden_part, "et", axis=1, tiled=True)
    expert_out = jnp.dot(piece, weight, preferred_element_type=jnp.float32)
    grad_weight = lax.dot_general(
        piece, scaled, (((0,), (0,)), ((), ())), preferred_element_type=jnp.float32
    )
    partial_grad = jnp.sum(rows_in.astype(jnp.float32) * expert_out, axis=1)
    slot_grad = lax.psum(partial_grad, "et")
    returned = lax.all_to_all(
        slot_grad.reshape(experts, capacity), "ep", split_axis=0, concat_axis=0, tiled=True
    )
    d_gate = returned.reshape(-1)[slot_of].reshape(tok_rows, topk)
    return (grad_weight.astype(jnp.bfloat16)[None], d_gate)


def solution(mesh):
    sizes = dict(mesh.shape)

    def local(out_grad, gate_weights, routes, gate_pre, up_pre, down_weight):
        tokens, topk = routes.shape
        whole = topk == sizes["ep"] and gate_pre.shape[1] == topk * tokens
        if whole and sizes["ep"] == 8 and sizes["et"] == 4:
            return dense(out_grad, gate_weights, routes, gate_pre, up_pre, down_weight)
        return routed(out_grad, gate_weights, routes, gate_pre, up_pre, down_weight)

    in_specs = (
        P("ep", "et"),
        P("ep", None),
        P("ep", None),
        P("ep", None, "et"),
        P("ep", None, "et"),
        P("ep", None, "et"),
    )
    out_specs = (P("ep", None, "et"), P("ep", None))
    return jax.shard_map(local, mesh=mesh, in_specs=in_specs, out_specs=out_specs, check_vma=False)
```

```python
import jax
import jax.numpy as jnp
from jax import lax
from jax.experimental import pallas as pl
from jax.experimental.pallas import tpu as pltpu
from jax.sharding import PartitionSpec as P

MIB = 1024 * 1024
BF16 = jnp.bfloat16
F32 = jnp.float32
LANES = 128


def vmem_spec():
    return pl.BlockSpec(memory_space=pltpu.VMEM)


def smem_spec():
    return pl.BlockSpec(memory_space=pltpu.SMEM)


def any_spec():
    return pl.BlockSpec(memory_space=pl.ANY)


def params(mib):
    return pltpu.CompilerParams(vmem_limit_bytes=mib * MIB)


def declared(flops=0):
    return pl.CostEstimate(flops=int(flops), bytes_accessed=1000, transcendentals=0)


def in_hbm(x):
    return pltpu.with_memory_space_constraint(x, pltpu.HBM)


def ring_of(experts):
    return list(range(0, experts, 2)) + list(range(experts - 1, 0, -2))


def source_of(me, step, experts):
    at = jnp.where(me % 2 == 0, me // 2, experts - 1 - me // 2)
    at = (at + step + experts) % experts
    return jnp.where(at < experts // 2, 2 * at, 2 * (experts - 1 - at) + 1)


def chunks_of(out_grad, gates_t, routes_t):
    tokens, feats = out_grad.shape
    experts = routes_t.shape[0]
    half = tokens // 2
    cols = feats // LANES

    def body(rows_ref, g_ref, r_ref, top_ref, bottom_ref):
        routes = r_ref[...]
        gates = g_ref[...].astype(F32)
        by = [
            jnp.sum(jnp.where(routes == e, gates, 0.0), axis=0, keepdims=True) for e in range(experts)
        ]
        by = jnp.concatenate(by + [jnp.zeros((16 - experts, tokens), F32)], axis=0).astype(BF16)
        for c, ref in enumerate((top_ref, bottom_ref)):
            for j in range(cols):
                ref[j * half : (j + 1) * half, :] = rows_ref[
                    c * half : (c + 1) * half, j * LANES : (j + 1) * LANES
                ]
            ref[cols * half :, :] = by

    operands = (out_grad, gates_t, routes_t)
    return pl.pallas_call(
        body,
        grid=(1,),
        in_specs=[pl.BlockSpec(x.shape, lambda i: (0, 0)) for x in operands],
        out_specs=[vmem_spec()] * 2,
        out_shape=[pltpu.VMEM((cols * half + 16, LANES), BF16)] * 2,
        compiler_params=params(4),
        cost_estimate=declared(),
        name="chunks",
    )(*[in_hbm(x) for x in operands])


def hidden_of(gate_pre, up_pre, weight):
    slots, width = gate_pre.shape
    blocks = 4
    rows = slots // blocks

    def body(pre_ref, up_ref, w_ref, hidden_ref, held_ref, pre_scr, up_scr, sems):
        copies = []
        for i in range(blocks):
            here = pl.ds(i * rows, rows)
            copies.append(
                [
                    pltpu.make_async_copy(src.at[here], dst.at[here], sems.at[2 * i + j])
                    for j, (src, dst) in enumerate(((pre_ref, pre_scr), (up_ref, up_scr)))
                ]
            )
        fetch = pltpu.make_async_copy(w_ref, held_ref, sems.at[2 * blocks])
        for copy in sum(copies, []):
            copy.start()
        fetch.start()
        for i in range(blocks):
            for copy in copies[i]:
                copy.wait()
            here = pl.ds(i * rows, rows)
            pre = pre_scr[here, :].astype(F32)
            hidden_ref[here, :] = (pre / (1.0 + jnp.exp(-pre)) * up_scr[here, :].astype(F32)).astype(BF16)
        fetch.wait()

    return pl.pallas_call(
        body,
        in_specs=[any_spec()] * 3,
        out_specs=[vmem_spec()] * 2,
        out_shape=[pltpu.VMEM((slots, width), BF16), pltpu.VMEM(weight.shape, BF16)],
        scratch_shapes=[
            pltpu.VMEM((slots, width), BF16),
            pltpu.VMEM((slots, width), BF16),
            pltpu.SemaphoreType.DMA((2 * blocks + 1,)),
        ],
        compiler_params=params(4),
        cost_estimate=declared(),
        name="hidden",
    )(*[in_hbm(x) for x in (gate_pre, up_pre, weight)])


def assemble(info, parts, weight, tokens, steps, feats):
    slots, width = parts[0].shape
    units = weight.shape[0]
    groups, experts = len(parts), slots // tokens
    cols = 256

    def body(info_ref, *refs):
        part_refs, (w_ref, h_ref, ht_ref, eo_ref) = refs[:groups], refs[groups:]
        for m, ref in enumerate(part_refs):
            at = pl.multiple_of((info_ref[0] ^ m) * width, width)
            for i, step in enumerate(steps):
                start = pl.multiple_of(source_of(info_ref[1], step, experts) * tokens, tokens)
                value = ref[pl.ds(start, tokens), :]
                here = slice(i * tokens, (i + 1) * tokens)
                h_ref[here, pl.ds(at, width)] = value
                ht_ref[pl.ds(at, width), here] = value.T
        for j in range(feats // cols):
            here = slice(j * cols, (j + 1) * cols)
            eo_ref[:, here] = jnp.dot(h_ref[...], w_ref[:, here], preferred_element_type=F32)

    return pl.pallas_call(
        body,
        in_specs=[smem_spec()] + [vmem_spec()] * (groups + 1),
        out_specs=[vmem_spec()] * 3,
        out_shape=[
            pltpu.VMEM((slots, units), BF16),
            pltpu.VMEM((units, slots), BF16),
            pltpu.VMEM((slots, feats), F32),
        ],
        compiler_params=params(6),
        cost_estimate=declared(),
        name="expert_out_first",
    )(info, *parts, weight)


def expert_out_rest(hidden, weight, scaled, feats):
    slots = hidden.shape[0]
    first, feats = feats, weight.shape[1]
    cols = 256
    counts = [x.shape[0] for x in scaled]

    def body(h_ref, w_ref, *refs):
        scaled_refs, (eo_ref, out_ref, sems) = refs[: len(scaled)], refs[len(scaled) :]
        copies = [
            pltpu.make_async_copy(ref, out_ref.at[pl.ds(sum(counts[:i]), counts[i])], sems.at[i])
            for i, ref in enumerate(scaled_refs)
        ]
        for copy in copies:
            copy.start()
        for j in range(first, feats, cols):
            eo_ref[:, j - first : j - first + cols] = jnp.dot(
                h_ref[...], w_ref[:, j : j + cols], preferred_element_type=F32
            )
        for copy in copies:
            copy.wait()

    return pl.pallas_call(
        body,
        in_specs=[vmem_spec()] * (2 + len(scaled)),
        out_specs=[vmem_spec(), any_spec()],
        out_shape=[pltpu.VMEM((slots, feats - first), F32), pltpu.HBM((sum(counts), feats), BF16)],
        scratch_shapes=[pltpu.SemaphoreType.DMA((len(scaled),))],
        compiler_params=params(6),
        cost_estimate=declared(),
        name="expert_out_rest",
    )(hidden, weight, *scaled)


def column(row):
    return jnp.broadcast_to(row, (8, row.shape[1])).T[:, :1]


def gate_of(chunk_ref, me, half, lower):
    by = chunk_ref[chunk_ref.shape[0] - 16 :, :].astype(F32)
    row = lax.broadcasted_iota(jnp.int32, by.shape, 0)
    gate = jnp.sum(jnp.where(row == me, by, 0.0), axis=0, keepdims=True)
    return column(gate)[lower * half : (lower + 1) * half]


def add_up(chunk_ref, eo_refs, at, half):
    total = jnp.zeros((half, LANES), F32)
    j = 0
    for ref in eo_refs:
        for k in range(ref.shape[1] // LANES):
            value = chunk_ref[j * half : (j + 1) * half, :].astype(F32)
            total = total + value * ref[at : at + half, k * LANES : (k + 1) * LANES]
            j += 1
    return jnp.sum(total, axis=1, keepdims=True)


def put_scaled(chunk_ref, out_ref, at, gate, half):
    for j in range(out_ref.shape[1] // LANES):
        value = chunk_ref[j * half : (j + 1) * half, :].astype(F32)
        out_ref[at : at + half, j * LANES : (j + 1) * LANES] = (value * gate).astype(BF16)


def scaled_rows(info, chunks, lowers, half, flops):
    cols = (chunks[0].shape[0] - 16) // half
    count = len(chunks)

    def body(info_ref, *refs):
        out_ref = refs[count]
        for i, ref in enumerate(refs[:count]):
            put_scaled(ref, out_ref, i * half, gate_of(ref, info_ref[1], half, lowers[i]), half)

    return pl.pallas_call(
        body,
        in_specs=[smem_spec()] + [vmem_spec()] * count,
        out_specs=vmem_spec(),
        out_shape=pltpu.VMEM((count * half, cols * LANES), BF16),
        compiler_params=params(3),
        cost_estimate=declared(flops),
        name="scaled_rows",
    )(info, *chunks)


def absorb(info, chunks, expert_out, tokens, steps):
    half = tokens // 2
    experts = expert_out[0].shape[0] // tokens
    count = len(chunks) // 2

    def body(info_ref, *refs):
        chunk_refs, eo_refs = refs[: 2 * count], refs[2 * count : 2 * count + 2]
        sums_ref, last_ref, own_ref = refs[2 * count + 2 :]
        me = info_ref[1]
        lanes = []
        for i in range(count):
            at = i * tokens
            sums = [add_up(chunk_refs[2 * i + c], eo_refs, at + c * half, half) for c in range(2)]
            lanes.append(jnp.concatenate(sums, axis=0))
        lanes += [jnp.zeros((tokens, 1), F32)] * (experts - count)
        by_step = jnp.concatenate(lanes, axis=1).T
        row = lax.broadcasted_iota(jnp.int32, (experts, tokens), 0)
        total = jnp.zeros((experts, tokens), F32)
        for i, step in enumerate(steps[:count]):
            total = jnp.where(row == source_of(me, step, experts), by_step[i : i + 1], total)
        sums_ref[...] = total
        last_ref[...] = (row == source_of(me, steps[-1], experts)).astype(F32)
        own_ref[...] = (lax.broadcasted_iota(jnp.int32, own_ref.shape, 0) == me).astype(F32)

    return pl.pallas_call(
        body,
        in_specs=[smem_spec()] + [vmem_spec()] * (2 * count + 2),
        out_specs=[vmem_spec()] * 3,
        out_shape=[
            pltpu.VMEM((experts, tokens), F32),
            pltpu.VMEM((experts, tokens), F32),
            pltpu.VMEM((16, LANES), F32),
        ],
        compiler_params=params(4),
        cost_estimate=declared(),
        name="absorb",
    )(info, *chunks, *expert_out)


def absorb_last(chunks, expert_out, sums, mask, groups):
    experts, tokens = sums.shape
    half = tokens // 2
    first = expert_out[0].shape[0] - tokens

    def body(top_ref, bottom_ref, eo_ref, rest_ref, sums_ref, mask_ref, out_ref):
        parts = [add_up(ref, (eo_ref, rest_ref), first + c * half, half) for c, ref in enumerate((top_ref, bottom_ref))]
        own = jnp.broadcast_to(jnp.concatenate(parts, axis=0), (tokens, experts)).T
        value = jnp.where(mask_ref[...] > 0.0, own, sums_ref[...])
        out_ref[...] = jnp.broadcast_to(value[:, None, :], out_ref.shape)

    return pl.pallas_call(
        body,
        in_specs=[vmem_spec()] * 6,
        out_specs=vmem_spec(),
        out_shape=jax.ShapeDtypeStruct((experts, groups, tokens), F32),
        compiler_params=params(2),
        cost_estimate=declared(),
        name="absorb_last",
    )(*chunks, *expert_out, sums, mask)


def weight_grad(own, early, early_places, late, late_places, last_chunks, hidden_t):
    units, slots = hidden_t.shape
    feats = late[0].shape[1]
    half = late[0].shape[0] // len(late_places[0])
    blocks = 4
    rows = units // blocks

    def body(own_ref, early_ref, *refs):
        late_refs, refs = refs[: len(late)], refs[len(late) :]
        top_ref, bottom_ref, ht_ref, out_ref, rows_scr, held, in_sems, out_sems = refs
        copies = [
            pltpu.make_async_copy(
                early_ref.at[pl.ds(i * half, half)], rows_scr.at[pl.ds(place, half)], in_sems.at[i]
            )
            for i, place in enumerate(early_places)
        ]
        for copy in copies:
            copy.start()
        for ref, at in zip(late_refs, late_places):
            for i, place in enumerate(at):
                rows_scr[place : place + half, :] = ref[i * half : (i + 1) * half, :]
        for c, ref in enumerate((top_ref, bottom_ref)):
            by = ref[ref.shape[0] - 16 :, :].astype(F32)
            gate = column(jnp.sum(by * own_ref[...], axis=0, keepdims=True))[c * half : (c + 1) * half]
            put_scaled(ref, rows_scr, slots - (2 - c) * half, gate, half)
        for copy in copies:
            copy.wait()
        copies = []
        for i in range(blocks):
            here = pl.ds(i * rows, rows)
            held[here, :] = jnp.dot(ht_ref[here, :], rows_scr[...], preferred_element_type=F32).astype(BF16)
            copy = pltpu.make_async_copy(held.at[here], out_ref.at[here], out_sems.at[i])
            copy.start()
            copies.append(copy)
        for copy in copies:
            copy.wait()

    return pl.pallas_call(
        body,
        in_specs=[vmem_spec(), any_spec()] + [vmem_spec()] * (3 + len(late)),
        out_specs=any_spec(),
        out_shape=jax.ShapeDtypeStruct((units, feats), BF16),
        scratch_shapes=[
            pltpu.VMEM((slots, feats), BF16),
            pltpu.VMEM((units, feats), BF16),
            pltpu.SemaphoreType.DMA((len(early_places),)),
            pltpu.SemaphoreType.DMA((blocks,)),
        ],
        compiler_params=params(12),
        cost_estimate=declared(),
        name="weight_grad",
    )(own, in_hbm(early), *late, *last_chunks, hidden_t)


def pick(returned, routes_t):
    topk, tokens = routes_t.shape
    experts, groups, _ = returned.shape

    def body(back_ref, routes_ref, out_ref):
        routes = routes_ref[...]
        total = jnp.zeros((topk, tokens), F32)
        for e in range(experts):
            value = jnp.sum(back_ref[e], axis=0, keepdims=True)
            total = jnp.where(routes == e, jnp.broadcast_to(value, total.shape), total)
        out_ref[...] = total

    return pl.pallas_call(
        body,
        in_specs=[vmem_spec(), vmem_spec()],
        out_specs=vmem_spec(),
        out_shape=jax.ShapeDtypeStruct((topk, tokens), F32),
        compiler_params=params(2),
        name="pick_gate_grad",
    )(returned, routes_t)


def dense(out_grad, gate_weights, routes, gate_pre, up_pre, down_weight):
    tokens, topk = routes.shape
    experts, groups = lax.axis_size("ep"), lax.axis_size("et")
    weight = down_weight[0]
    barrier = lax.optimization_barrier

    ring = ring_of(experts)
    forth = [(ring[i], ring[(i + 1) % experts]) for i in range(experts)]
    back = [(b, a) for a, b in forth]
    far = experts // 2
    steps = [0] + [s for k in range(1, far) for s in (-k, k)] + [far]
    info = jnp.stack([lax.axis_index("et").astype(jnp.int32), lax.axis_index("ep").astype(jnp.int32)])
    out_grad, info = barrier((out_grad, info))

    top, bottom = chunks_of(out_grad, gate_weights.T, routes.T)
    hidden, weight = hidden_of(gate_pre[0], up_pre[0], weight)
    chips, cores = [(i, i ^ 2) for i in range(groups)], [(i, i ^ 1) for i in range(groups)]
    half = tokens // 2

    def hop(c):
        up[c] = lax.ppermute(up[c], "ep", forth)
        down[c] = lax.ppermute(down[c], "ep", back)

    def scale(chunks, lowers, flops=0):
        return scaled_rows(info, chunks, lowers, half, flops)

    up, down = [top, bottom], [bottom, top]
    hop(0)
    hop(1)
    over = lax.ppermute(hidden, "et", chips)
    beside, across = lax.ppermute(hidden, "et", cores), lax.ppermute(over, "et", cores)
    up[0], down[0] = barrier((up[0], down[0]))
    first = [up[0], up[1], down[1], down[0]]
    hop(0)
    hop(1)
    second = [up[0], up[1], down[1], down[0]]
    scaled_a = scale([top, bottom] + first, [0, 1] * 3, 4e9)
    up[0], down[0], scaled_a = barrier((up[0], down[0], scaled_a))
    hop(0)
    scaled_b = scale(second, [0, 1] * 2, 8e9)
    up[1], down[1], scaled_b = barrier((up[1], down[1], scaled_b))
    hop(1)
    cut = weight.shape[1] // 256 * 3 // 7 * 256
    hidden, hidden_t, start = assemble(info, [hidden, beside, over, across], weight, tokens, steps, cut)
    up[0], down[0], hidden_t = barrier((up[0], down[0], hidden_t))
    third = [up[0], up[1], down[1], down[0]]
    scaled_c = scale([up[0], down[0]], [0, 1], 12e9)
    up[0], down[0], scaled_c = barrier((up[0], down[0], scaled_c))

    hop(0)
    rest, early = expert_out_rest(hidden, weight, [scaled_a, scaled_b], cut)
    expert_out = [start, rest]
    third, early = barrier((third, early))
    scaled_d = scale([third[1], third[2]], [1, 0])
    third, scaled_d = barrier((third, scaled_d))
    sums, mask, own = absorb(info, [top, bottom] + first + second + third, expert_out, tokens, steps)
    outgoing = absorb_last([up[0], down[0]], expert_out, sums, mask, groups)
    returned = lax.all_to_all(
        outgoing.reshape(experts * groups, tokens), ("ep", "et"), split_axis=0, concat_axis=0, tiled=True
    )
    late_places = [[10 * half, 13 * half], [11 * half, 12 * half]]
    grad = weight_grad(
        own, early, [i * half for i in range(10)], [scaled_c, scaled_d], late_places, [up[0], down[0]], hidden_t
    )
    d_gate = pick(returned.reshape(experts, groups, tokens), routes.T).T
    return grad[None], d_gate


def routed(out_grad, gate_weights, routes, gate_pre, up_pre, down_weight):
    tok_rows, topk = routes.shape
    experts = lax.axis_size("ep")
    slot_total = gate_pre.shape[1]
    capacity = slot_total // experts
    flat_route = routes.reshape(-1)
    pair_count = tok_rows * topk
    onehot = (flat_route[:, None] == jnp.arange(experts, dtype=jnp.int32)[None, :]).astype(
        jnp.int32
    )
    ranks = jnp.sum(jnp.cumsum(onehot, axis=0) * onehot, axis=1) - 1
    slot_of = flat_route * capacity + ranks
    pair_ids = jnp.arange(pair_count, dtype=jnp.int32)
    slot_pair = jnp.zeros((experts * capacity,), jnp.int32).at[slot_of].set(pair_ids)
    filled = jnp.zeros((experts * capacity,), jnp.bool_).at[slot_of].set(True)
    send_rows = jnp.where(filled[:, None], out_grad[slot_pair // topk], 0.0)
    send_rows = send_rows.reshape(experts, capacity, out_grad.shape[1])
    send_gates = jnp.where(filled, gate_weights.reshape(-1)[slot_pair], 0.0)
    send_gates = send_gates.reshape(experts, capacity)
    rows_in, gates_in = (
        lax.all_to_all(send_rows, "ep", split_axis=0, concat_axis=0, tiled=True),
        lax.all_to_all(send_gates, "ep", split_axis=0, concat_axis=0, tiled=True),
    )
    rows_in = rows_in.reshape(slot_total, out_grad.shape[1])
    gates_in = gates_in.reshape(slot_total)
    weight = down_weight[0]
    hidden_part = (
        jax.nn.silu(gate_pre[0].astype(jnp.float32)) * up_pre[0].astype(jnp.float32)
    ).astype(jnp.bfloat16)
    scaled = (gates_in.astype(jnp.float32)[:, None] * rows_in.astype(jnp.float32)).astype(
        jnp.bfloat16
    )
    piece = lax.all_gather(hidden_part, "et", axis=1, tiled=True)
    expert_out = jnp.dot(piece, weight, preferred_element_type=jnp.float32)
    grad_weight = lax.dot_general(
        piece, scaled, (((0,), (0,)), ((), ())), preferred_element_type=jnp.float32
    )
    partial_grad = jnp.sum(rows_in.astype(jnp.float32) * expert_out, axis=1)
    slot_grad = lax.psum(partial_grad, "et")
    returned = lax.all_to_all(
        slot_grad.reshape(experts, capacity), "ep", split_axis=0, concat_axis=0, tiled=True
    )
    d_gate = returned.reshape(-1)[slot_of].reshape(tok_rows, topk)
    return (grad_weight.astype(jnp.bfloat16)[None], d_gate)


def solution(mesh):
    sizes = dict(mesh.shape)

    def local(out_grad, gate_weights, routes, gate_pre, up_pre, down_weight):
        tokens, topk = routes.shape
        whole = topk == sizes["ep"] and gate_pre.shape[1] == topk * tokens
        if whole and sizes["ep"] == 8 and sizes["et"] == 4:
            return dense(out_grad, gate_weights, routes, gate_pre, up_pre, down_weight)
        return routed(out_grad, gate_weights, routes, gate_pre, up_pre, down_weight)

    in_specs = (
        P("ep", "et"),
        P("ep", None),
        P("ep", None),
        P("ep", None, "et"),
        P("ep", None, "et"),
        P("ep", None, "et"),
    )
    out_specs = (P("ep", None, "et"), P("ep", None))
    return jax.shard_map(local, mesh=mesh, in_specs=in_specs, out_specs=out_specs, check_vma=False)
```

```python
import jax
import jax.numpy as jnp
from jax import lax
from jax.experimental import pallas as pl
from jax.experimental.pallas import tpu as pltpu
from jax.sharding import PartitionSpec as P

MIB = 1024 * 1024
BF16 = jnp.bfloat16
F32 = jnp.float32
LANES = 128


def vmem_spec():
    return pl.BlockSpec(memory_space=pltpu.VMEM)


def smem_spec():
    return pl.BlockSpec(memory_space=pltpu.SMEM)


def any_spec():
    return pl.BlockSpec(memory_space=pl.ANY)


def params(mib):
    return pltpu.CompilerParams(vmem_limit_bytes=mib * MIB)


def declared(flops=0):
    return pl.CostEstimate(flops=int(flops), bytes_accessed=1000, transcendentals=0)


def in_hbm(x):
    return pltpu.with_memory_space_constraint(x, pltpu.HBM)


def ring_of(experts):
    return list(range(0, experts, 2)) + list(range(experts - 1, 0, -2))


def source_of(me, step, experts):
    at = jnp.where(me % 2 == 0, me // 2, experts - 1 - me // 2)
    at = (at + step + experts) % experts
    return jnp.where(at < experts // 2, 2 * at, 2 * (experts - 1 - at) + 1)


def chunks_of(out_grad, gates_t, routes_t):
    tokens, feats = out_grad.shape
    experts = routes_t.shape[0]
    half = tokens // 2
    cols = feats // LANES

    def body(rows_ref, g_ref, r_ref, top_ref, bottom_ref):
        routes = r_ref[...]
        gates = g_ref[...].astype(F32)
        by = [
            jnp.sum(jnp.where(routes == e, gates, 0.0), axis=0, keepdims=True) for e in range(experts)
        ]
        by = jnp.concatenate(by + [jnp.zeros((16 - experts, tokens), F32)], axis=0).astype(BF16)
        for c, ref in enumerate((top_ref, bottom_ref)):
            for j in range(cols):
                ref[j * half : (j + 1) * half, :] = rows_ref[
                    c * half : (c + 1) * half, j * LANES : (j + 1) * LANES
                ]
            ref[cols * half :, :] = by

    operands = (out_grad, gates_t, routes_t)
    return pl.pallas_call(
        body,
        grid=(1,),
        in_specs=[pl.BlockSpec(x.shape, lambda i: (0, 0)) for x in operands],
        out_specs=[vmem_spec()] * 2,
        out_shape=[pltpu.VMEM((cols * half + 16, LANES), BF16)] * 2,
        compiler_params=params(4),
        cost_estimate=declared(),
        name="chunks",
    )(*[in_hbm(x) for x in operands])


def hidden_of(gate_pre, up_pre, weight):
    slots, width = gate_pre.shape
    blocks = 4
    rows = slots // blocks

    def body(pre_ref, up_ref, w_ref, hidden_ref, held_ref, pre_scr, up_scr, sems):
        copies = []
        for i in range(blocks):
            here = pl.ds(i * rows, rows)
            copies.append(
                [
                    pltpu.make_async_copy(src.at[here], dst.at[here], sems.at[2 * i + j])
                    for j, (src, dst) in enumerate(((pre_ref, pre_scr), (up_ref, up_scr)))
                ]
            )
        fetch = pltpu.make_async_copy(w_ref, held_ref, sems.at[2 * blocks])
        for copy in sum(copies, []):
            copy.start()
        fetch.start()
        for i in range(blocks):
            for copy in copies[i]:
                copy.wait()
            here = pl.ds(i * rows, rows)
            pre = pre_scr[here, :].astype(F32)
            hidden_ref[here, :] = (pre / (1.0 + jnp.exp(-pre)) * up_scr[here, :].astype(F32)).astype(BF16)
        fetch.wait()

    return pl.pallas_call(
        body,
        in_specs=[any_spec()] * 3,
        out_specs=[vmem_spec()] * 2,
        out_shape=[pltpu.VMEM((slots, width), BF16), pltpu.VMEM(weight.shape, BF16)],
        scratch_shapes=[
            pltpu.VMEM((slots, width), BF16),
            pltpu.VMEM((slots, width), BF16),
            pltpu.SemaphoreType.DMA((2 * blocks + 1,)),
        ],
        compiler_params=params(4),
        cost_estimate=declared(),
        name="hidden",
    )(*[in_hbm(x) for x in (gate_pre, up_pre, weight)])


def assemble(info, parts, weight, tokens, steps, feats):
    slots, width = parts[0].shape
    units = weight.shape[0]
    groups, experts = len(parts), slots // tokens
    cols = 256

    def body(info_ref, *refs):
        part_refs, (w_ref, h_ref, ht_ref, eo_ref) = refs[:groups], refs[groups:]
        for m, ref in enumerate(part_refs):
            at = pl.multiple_of((info_ref[0] ^ m) * width, width)
            for i, step in enumerate(steps):
                start = pl.multiple_of(source_of(info_ref[1], step, experts) * tokens, tokens)
                value = ref[pl.ds(start, tokens), :]
                here = slice(i * tokens, (i + 1) * tokens)
                h_ref[here, pl.ds(at, width)] = value
                ht_ref[pl.ds(at, width), here] = value.T
        for j in range(feats // cols):
            here = slice(j * cols, (j + 1) * cols)
            eo_ref[:, here] = jnp.dot(h_ref[...], w_ref[:, here], preferred_element_type=F32)

    return pl.pallas_call(
        body,
        in_specs=[smem_spec()] + [vmem_spec()] * (groups + 1),
        out_specs=[vmem_spec()] * 3,
        out_shape=[
            pltpu.VMEM((slots, units), BF16),
            pltpu.VMEM((units, slots), BF16),
            pltpu.VMEM((slots, feats), F32),
        ],
        compiler_params=params(6),
        cost_estimate=declared(),
        name="expert_out_first",
    )(info, *parts, weight)


def expert_out_rest(hidden, weight, scaled, feats):
    slots = hidden.shape[0]
    first, feats = feats, weight.shape[1]
    cols = 256
    counts = [x.shape[0] for x in scaled]

    def body(h_ref, w_ref, *refs):
        scaled_refs, (eo_ref, out_ref, sems) = refs[: len(scaled)], refs[len(scaled) :]
        copies = [
            pltpu.make_async_copy(ref, out_ref.at[pl.ds(sum(counts[:i]), counts[i])], sems.at[i])
            for i, ref in enumerate(scaled_refs)
        ]
        for copy in copies:
            copy.start()
        for j in range(first, feats, cols):
            eo_ref[:, j - first : j - first + cols] = jnp.dot(
                h_ref[...], w_ref[:, j : j + cols], preferred_element_type=F32
            )
        for copy in copies:
            copy.wait()

    return pl.pallas_call(
        body,
        in_specs=[vmem_spec()] * (2 + len(scaled)),
        out_specs=[vmem_spec(), any_spec()],
        out_shape=[pltpu.VMEM((slots, feats - first), F32), pltpu.HBM((sum(counts), feats), BF16)],
        scratch_shapes=[pltpu.SemaphoreType.DMA((len(scaled),))],
        compiler_params=params(6),
        cost_estimate=declared(),
        name="expert_out_rest",
    )(hidden, weight, *scaled)


def column(row):
    return jnp.broadcast_to(row, (8, row.shape[1])).T[:, :1]


def gate_of(chunk_ref, me, half, lower):
    by = chunk_ref[chunk_ref.shape[0] - 16 :, :].astype(F32)
    row = lax.broadcasted_iota(jnp.int32, by.shape, 0)
    gate = jnp.sum(jnp.where(row == me, by, 0.0), axis=0, keepdims=True)
    return column(gate)[lower * half : (lower + 1) * half]


def add_up(chunk_ref, eo_refs, at, half):
    total = jnp.zeros((half, LANES), F32)
    j = 0
    for ref in eo_refs:
        for k in range(ref.shape[1] // LANES):
            value = chunk_ref[j * half : (j + 1) * half, :].astype(F32)
            total = total + value * ref[at : at + half, k * LANES : (k + 1) * LANES]
            j += 1
    return jnp.sum(total, axis=1, keepdims=True)


def put_scaled(chunk_ref, out_ref, at, gate, half):
    for j in range(out_ref.shape[1] // LANES):
        value = chunk_ref[j * half : (j + 1) * half, :].astype(F32)
        out_ref[at : at + half, j * LANES : (j + 1) * LANES] = (value * gate).astype(BF16)


def scaled_rows(info, chunks, lowers, half, flops):
    cols = (chunks[0].shape[0] - 16) // half
    count = len(chunks)

    def body(info_ref, *refs):
        out_ref = refs[count]
        for i, ref in enumerate(refs[:count]):
            put_scaled(ref, out_ref, i * half, gate_of(ref, info_ref[1], half, lowers[i]), half)

    return pl.pallas_call(
        body,
        in_specs=[smem_spec()] + [vmem_spec()] * count,
        out_specs=vmem_spec(),
        out_shape=pltpu.VMEM((count * half, cols * LANES), BF16),
        compiler_params=params(3),
        cost_estimate=declared(flops),
        name="scaled_rows",
    )(info, *chunks)


def absorb(info, chunks, expert_out, tokens, steps):
    half = tokens // 2
    experts = expert_out[0].shape[0] // tokens
    count = len(chunks) // 2

    def body(info_ref, *refs):
        chunk_refs, eo_refs = refs[: 2 * count], refs[2 * count : 2 * count + 2]
        sums_ref, last_ref, own_ref = refs[2 * count + 2 :]
        me = info_ref[1]
        lanes = []
        for i in range(count):
            at = i * tokens
            sums = [add_up(chunk_refs[2 * i + c], eo_refs, at + c * half, half) for c in range(2)]
            lanes.append(jnp.concatenate(sums, axis=0))
        lanes += [jnp.zeros((tokens, 1), F32)] * (experts - count)
        by_step = jnp.concatenate(lanes, axis=1).T
        row = lax.broadcasted_iota(jnp.int32, (experts, tokens), 0)
        total = jnp.zeros((experts, tokens), F32)
        for i, step in enumerate(steps[:count]):
            total = jnp.where(row == source_of(me, step, experts), by_step[i : i + 1], total)
        sums_ref[...] = total
        last_ref[...] = (row == source_of(me, steps[-1], experts)).astype(F32)
        own_ref[...] = (lax.broadcasted_iota(jnp.int32, own_ref.shape, 0) == me).astype(F32)

    return pl.pallas_call(
        body,
        in_specs=[smem_spec()] + [vmem_spec()] * (2 * count + 2),
        out_specs=[vmem_spec()] * 3,
        out_shape=[
            pltpu.VMEM((experts, tokens), F32),
            pltpu.VMEM((experts, tokens), F32),
            pltpu.VMEM((16, LANES), F32),
        ],
        compiler_params=params(4),
        cost_estimate=declared(),
        name="absorb",
    )(info, *chunks, *expert_out)


def absorb_last(chunks, expert_out, sums, mask, groups):
    experts, tokens = sums.shape
    half = tokens // 2
    first = expert_out[0].shape[0] - tokens

    def body(top_ref, bottom_ref, eo_ref, rest_ref, sums_ref, mask_ref, out_ref):
        parts = [add_up(ref, (eo_ref, rest_ref), first + c * half, half) for c, ref in enumerate((top_ref, bottom_ref))]
        own = jnp.broadcast_to(jnp.concatenate(parts, axis=0), (tokens, experts)).T
        value = jnp.where(mask_ref[...] > 0.0, own, sums_ref[...])
        out_ref[...] = jnp.broadcast_to(value[:, None, :], out_ref.shape)

    return pl.pallas_call(
        body,
        in_specs=[vmem_spec()] * 6,
        out_specs=vmem_spec(),
        out_shape=jax.ShapeDtypeStruct((experts, groups, tokens), F32),
        compiler_params=params(2),
        cost_estimate=declared(),
        name="absorb_last",
    )(*chunks, *expert_out, sums, mask)


def weight_grad(own, early, early_places, late, late_places, last_chunks, hidden_t):
    units, slots = hidden_t.shape
    feats = late[0].shape[1]
    half = late[0].shape[0] // len(late_places[0])
    blocks = 4
    rows = units // blocks

    def body(own_ref, early_ref, *refs):
        late_refs, refs = refs[: len(late)], refs[len(late) :]
        top_ref, bottom_ref, ht_ref, out_ref, rows_scr, held, in_sems, out_sems = refs
        copies = [
            pltpu.make_async_copy(
                early_ref.at[pl.ds(i * half, half)], rows_scr.at[pl.ds(place, half)], in_sems.at[i]
            )
            for i, place in enumerate(early_places)
        ]
        for copy in copies:
            copy.start()
        for ref, at in zip(late_refs, late_places):
            for i, place in enumerate(at):
                rows_scr[place : place + half, :] = ref[i * half : (i + 1) * half, :]
        for c, ref in enumerate((top_ref, bottom_ref)):
            by = ref[ref.shape[0] - 16 :, :].astype(F32)
            gate = column(jnp.sum(by * own_ref[...], axis=0, keepdims=True))[c * half : (c + 1) * half]
            put_scaled(ref, rows_scr, slots - (2 - c) * half, gate, half)
        for copy in copies:
            copy.wait()
        copies = []
        for i in range(blocks):
            here = pl.ds(i * rows, rows)
            held[here, :] = jnp.dot(ht_ref[here, :], rows_scr[...], preferred_element_type=F32).astype(BF16)
            copy = pltpu.make_async_copy(held.at[here], out_ref.at[here], out_sems.at[i])
            copy.start()
            copies.append(copy)
        for copy in copies:
            copy.wait()

    return pl.pallas_call(
        body,
        in_specs=[vmem_spec(), any_spec()] + [vmem_spec()] * (3 + len(late)),
        out_specs=any_spec(),
        out_shape=jax.ShapeDtypeStruct((units, feats), BF16),
        scratch_shapes=[
            pltpu.VMEM((slots, feats), BF16),
            pltpu.VMEM((units, feats), BF16),
            pltpu.SemaphoreType.DMA((len(early_places),)),
            pltpu.SemaphoreType.DMA((blocks,)),
        ],
        compiler_params=params(12),
        cost_estimate=declared(),
        name="weight_grad",
    )(own, in_hbm(early), *late, *last_chunks, hidden_t)


def pick(returned, routes_t):
    topk, tokens = routes_t.shape
    experts, groups, _ = returned.shape

    def body(back_ref, routes_ref, out_ref):
        routes = routes_ref[...]
        total = jnp.zeros((topk, tokens), F32)
        for e in range(experts):
            value = jnp.sum(back_ref[e], axis=0, keepdims=True)
            total = jnp.where(routes == e, jnp.broadcast_to(value, total.shape), total)
        out_ref[...] = total

    return pl.pallas_call(
        body,
        in_specs=[vmem_spec(), vmem_spec()],
        out_specs=vmem_spec(),
        out_shape=jax.ShapeDtypeStruct((topk, tokens), F32),
        compiler_params=params(2),
        name="pick_gate_grad",
    )(returned, routes_t)


def dense(out_grad, gate_weights, routes, gate_pre, up_pre, down_weight):
    tokens, topk = routes.shape
    experts, groups = lax.axis_size("ep"), lax.axis_size("et")
    weight = down_weight[0]
    barrier = lax.optimization_barrier

    ring = ring_of(experts)
    forth = [(ring[i], ring[(i + 1) % experts]) for i in range(experts)]
    back = [(b, a) for a, b in forth]
    far = experts // 2
    steps = [0] + [s for k in range(1, far) for s in (-k, k)] + [far]
    info = jnp.stack([lax.axis_index("et").astype(jnp.int32), lax.axis_index("ep").astype(jnp.int32)])
    out_grad, info = barrier((out_grad, info))

    top, bottom = chunks_of(out_grad, gate_weights.T, routes.T)
    hidden, weight = hidden_of(gate_pre[0], up_pre[0], weight)
    chips, cores = [(i, i ^ 2) for i in range(groups)], [(i, i ^ 1) for i in range(groups)]
    half = tokens // 2

    def hop(c):
        up[c] = lax.ppermute(up[c], "ep", forth)
        down[c] = lax.ppermute(down[c], "ep", back)

    def scale(chunks, lowers, flops=0):
        return scaled_rows(info, chunks, lowers, half, flops)

    up, down = [top, bottom], [bottom, top]
    hop(0)
    hop(1)
    over = lax.ppermute(hidden, "et", chips)
    beside, across = lax.ppermute(hidden, "et", cores), lax.ppermute(over, "et", cores)
    up[0], down[0] = barrier((up[0], down[0]))
    first = [up[0], up[1], down[1], down[0]]
    hop(0)
    hop(1)
    second = [up[0], up[1], down[1], down[0]]
    scaled_a = scale([top, bottom] + first, [0, 1] * 3, 4e9)
    up[0], down[0], scaled_a = barrier((up[0], down[0], scaled_a))
    hop(0)
    scaled_b = scale(second, [0, 1] * 2, 8e9)
    up[1], down[1], scaled_b = barrier((up[1], down[1], scaled_b))
    hop(1)
    cut = weight.shape[1] // 256 * 4 // 7 * 256
    hidden, hidden_t, start = assemble(info, [hidden, beside, over, across], weight, tokens, steps, cut)
    up[0], down[0], hidden_t = barrier((up[0], down[0], hidden_t))
    third = [up[0], up[1], down[1], down[0]]
    scaled_c = scale([up[0], down[0]], [0, 1], 12e9)
    up[0], down[0], scaled_c = barrier((up[0], down[0], scaled_c))

    hop(0)
    rest, early = expert_out_rest(hidden, weight, [scaled_a, scaled_b], cut)
    expert_out = [start, rest]
    third, early = barrier((third, early))
    scaled_d = scale([third[1], third[2]], [1, 0])
    third, scaled_d = barrier((third, scaled_d))
    sums, mask, own = absorb(info, [top, bottom] + first + second + third, expert_out, tokens, steps)
    outgoing = absorb_last([up[0], down[0]], expert_out, sums, mask, groups)
    returned = lax.all_to_all(
        outgoing.reshape(experts * groups, tokens), ("ep", "et"), split_axis=0, concat_axis=0, tiled=True
    )
    late_places = [[10 * half, 13 * half], [11 * half, 12 * half]]
    grad = weight_grad(
        own, early, [i * half for i in range(10)], [scaled_c, scaled_d], late_places, [up[0], down[0]], hidden_t
    )
    d_gate = pick(returned.reshape(experts, groups, tokens), routes.T).T
    return grad[None], d_gate


def routed(out_grad, gate_weights, routes, gate_pre, up_pre, down_weight):
    tok_rows, topk = routes.shape
    experts = lax.axis_size("ep")
    slot_total = gate_pre.shape[1]
    capacity = slot_total // experts
    flat_route = routes.reshape(-1)
    pair_count = tok_rows * topk
    onehot = (flat_route[:, None] == jnp.arange(experts, dtype=jnp.int32)[None, :]).astype(
        jnp.int32
    )
    ranks = jnp.sum(jnp.cumsum(onehot, axis=0) * onehot, axis=1) - 1
    slot_of = flat_route * capacity + ranks
    pair_ids = jnp.arange(pair_count, dtype=jnp.int32)
    slot_pair = jnp.zeros((experts * capacity,), jnp.int32).at[slot_of].set(pair_ids)
    filled = jnp.zeros((experts * capacity,), jnp.bool_).at[slot_of].set(True)
    send_rows = jnp.where(filled[:, None], out_grad[slot_pair // topk], 0.0)
    send_rows = send_rows.reshape(experts, capacity, out_grad.shape[1])
    send_gates = jnp.where(filled, gate_weights.reshape(-1)[slot_pair], 0.0)
    send_gates = send_gates.reshape(experts, capacity)
    rows_in, gates_in = (
        lax.all_to_all(send_rows, "ep", split_axis=0, concat_axis=0, tiled=True),
        lax.all_to_all(send_gates, "ep", split_axis=0, concat_axis=0, tiled=True),
    )
    rows_in = rows_in.reshape(slot_total, out_grad.shape[1])
    gates_in = gates_in.reshape(slot_total)
    weight = down_weight[0]
    hidden_part = (
        jax.nn.silu(gate_pre[0].astype(jnp.float32)) * up_pre[0].astype(jnp.float32)
    ).astype(jnp.bfloat16)
    scaled = (gates_in.astype(jnp.float32)[:, None] * rows_in.astype(jnp.float32)).astype(
        jnp.bfloat16
    )
    piece = lax.all_gather(hidden_part, "et", axis=1, tiled=True)
    expert_out = jnp.dot(piece, weight, preferred_element_type=jnp.float32)
    grad_weight = lax.dot_general(
        piece, scaled, (((0,), (0,)), ((), ())), preferred_element_type=jnp.float32
    )
    partial_grad = jnp.sum(rows_in.astype(jnp.float32) * expert_out, axis=1)
    slot_grad = lax.psum(partial_grad, "et")
    returned = lax.all_to_all(
        slot_grad.reshape(experts, capacity), "ep", split_axis=0, concat_axis=0, tiled=True
    )
    d_gate = returned.reshape(-1)[slot_of].reshape(tok_rows, topk)
    return (grad_weight.astype(jnp.bfloat16)[None], d_gate)


def solution(mesh):
    sizes = dict(mesh.shape)

    def local(out_grad, gate_weights, routes, gate_pre, up_pre, down_weight):
        tokens, topk = routes.shape
        whole = topk == sizes["ep"] and gate_pre.shape[1] == topk * tokens
        if whole and sizes["ep"] == 8 and sizes["et"] == 4:
            return dense(out_grad, gate_weights, routes, gate_pre, up_pre, down_weight)
        return routed(out_grad, gate_weights, routes, gate_pre, up_pre, down_weight)

    in_specs = (
        P("ep", "et"),
        P("ep", None),
        P("ep", None),
        P("ep", None, "et"),
        P("ep", None, "et"),
        P("ep", None, "et"),
    )
    out_specs = (P("ep", None, "et"), P("ep", None))
    return jax.shard_map(local, mesh=mesh, in_specs=in_specs, out_specs=out_specs, check_vma=False)
```

```python
import jax
import jax.numpy as jnp
from jax import lax
from jax.experimental import pallas as pl
from jax.experimental.pallas import tpu as pltpu
from jax.sharding import PartitionSpec as P

MIB = 1024 * 1024
BF16 = jnp.bfloat16
F32 = jnp.float32
LANES = 128


def vmem_spec():
    return pl.BlockSpec(memory_space=pltpu.VMEM)


def smem_spec():
    return pl.BlockSpec(memory_space=pltpu.SMEM)


def any_spec():
    return pl.BlockSpec(memory_space=pl.ANY)


def params(mib):
    return pltpu.CompilerParams(vmem_limit_bytes=mib * MIB)


def declared(flops=0):
    return pl.CostEstimate(flops=int(flops), bytes_accessed=1000, transcendentals=0)


def in_hbm(x):
    return pltpu.with_memory_space_constraint(x, pltpu.HBM)


def ring_of(experts):
    return list(range(0, experts, 2)) + list(range(experts - 1, 0, -2))


def source_of(me, step, experts):
    at = jnp.where(me % 2 == 0, me // 2, experts - 1 - me // 2)
    at = (at + step + experts) % experts
    return jnp.where(at < experts // 2, 2 * at, 2 * (experts - 1 - at) + 1)


def chunks_of(out_grad, gates_t, routes_t):
    tokens, feats = out_grad.shape
    experts = routes_t.shape[0]
    half = tokens // 2
    cols = feats // LANES

    def body(rows_ref, g_ref, r_ref, top_ref, bottom_ref):
        routes = r_ref[...]
        gates = g_ref[...].astype(F32)
        by = [
            jnp.sum(jnp.where(routes == e, gates, 0.0), axis=0, keepdims=True) for e in range(experts)
        ]
        by = jnp.concatenate(by + [jnp.zeros((16 - experts, tokens), F32)], axis=0).astype(BF16)
        for c, ref in enumerate((top_ref, bottom_ref)):
            for j in range(cols):
                ref[j * half : (j + 1) * half, :] = rows_ref[
                    c * half : (c + 1) * half, j * LANES : (j + 1) * LANES
                ]
            ref[cols * half :, :] = by

    operands = (out_grad, gates_t, routes_t)
    return pl.pallas_call(
        body,
        grid=(1,),
        in_specs=[pl.BlockSpec(x.shape, lambda i: (0, 0)) for x in operands],
        out_specs=[vmem_spec()] * 2,
        out_shape=[pltpu.VMEM((cols * half + 16, LANES), BF16)] * 2,
        compiler_params=params(4),
        cost_estimate=declared(),
        name="chunks",
    )(*[in_hbm(x) for x in operands])


def hidden_of(gate_pre, up_pre, weight):
    slots, width = gate_pre.shape
    blocks = 4
    rows = slots // blocks

    def body(pre_ref, up_ref, w_ref, hidden_ref, held_ref, pre_scr, up_scr, sems):
        copies = []
        for i in range(blocks):
            here = pl.ds(i * rows, rows)
            copies.append(
                [
                    pltpu.make_async_copy(src.at[here], dst.at[here], sems.at[2 * i + j])
                    for j, (src, dst) in enumerate(((pre_ref, pre_scr), (up_ref, up_scr)))
                ]
            )
        fetch = pltpu.make_async_copy(w_ref, held_ref, sems.at[2 * blocks])
        for copy in sum(copies, []):
            copy.start()
        fetch.start()
        for i in range(blocks):
            for copy in copies[i]:
                copy.wait()
            here = pl.ds(i * rows, rows)
            pre = pre_scr[here, :].astype(F32)
            hidden_ref[here, :] = (pre / (1.0 + jnp.exp(-pre)) * up_scr[here, :].astype(F32)).astype(BF16)
        fetch.wait()

    return pl.pallas_call(
        body,
        in_specs=[any_spec()] * 3,
        out_specs=[vmem_spec()] * 2,
        out_shape=[pltpu.VMEM((slots, width), BF16), pltpu.VMEM(weight.shape, BF16)],
        scratch_shapes=[
            pltpu.VMEM((slots, width), BF16),
            pltpu.VMEM((slots, width), BF16),
            pltpu.SemaphoreType.DMA((2 * blocks + 1,)),
        ],
        compiler_params=params(4),
        cost_estimate=declared(),
        name="hidden",
    )(*[in_hbm(x) for x in (gate_pre, up_pre, weight)])


def assemble(info, parts, weight, tokens, steps, feats):
    slots, width = parts[0].shape
    units = weight.shape[0]
    groups, experts = len(parts), slots // tokens
    cols = 256

    def body(info_ref, *refs):
        part_refs, (w_ref, h_ref, ht_ref, eo_ref) = refs[:groups], refs[groups:]
        for m, ref in enumerate(part_refs):
            at = pl.multiple_of((info_ref[0] ^ m) * width, width)
            for i, step in enumerate(steps):
                start = pl.multiple_of(source_of(info_ref[1], step, experts) * tokens, tokens)
                value = ref[pl.ds(start, tokens), :]
                here = slice(i * tokens, (i + 1) * tokens)
                h_ref[here, pl.ds(at, width)] = value
                ht_ref[pl.ds(at, width), here] = value.T
        for j in range(feats // cols):
            here = slice(j * cols, (j + 1) * cols)
            eo_ref[:, here] = jnp.dot(h_ref[...], w_ref[:, here], preferred_element_type=F32)

    return pl.pallas_call(
        body,
        in_specs=[smem_spec()] + [vmem_spec()] * (groups + 1),
        out_specs=[vmem_spec()] * 3,
        out_shape=[
            pltpu.VMEM((slots, units), BF16),
            pltpu.VMEM((units, slots), BF16),
            pltpu.VMEM((slots, feats), F32),
        ],
        compiler_params=params(6),
        cost_estimate=declared(),
        name="expert_out_first",
    )(info, *parts, weight)


def expert_out_rest(hidden, weight, scaled, feats):
    slots = hidden.shape[0]
    first, feats = feats, weight.shape[1]
    cols = 256
    counts = [x.shape[0] for x in scaled]

    def body(h_ref, w_ref, *refs):
        scaled_refs, (eo_ref, out_ref, sems) = refs[: len(scaled)], refs[len(scaled) :]
        copies = [
            pltpu.make_async_copy(ref, out_ref.at[pl.ds(sum(counts[:i]), counts[i])], sems.at[i])
            for i, ref in enumerate(scaled_refs)
        ]
        for copy in copies:
            copy.start()
        for j in range(first, feats, cols):
            eo_ref[:, j - first : j - first + cols] = jnp.dot(
                h_ref[...], w_ref[:, j : j + cols], preferred_element_type=F32
            )
        for copy in copies:
            copy.wait()

    return pl.pallas_call(
        body,
        in_specs=[vmem_spec()] * (2 + len(scaled)),
        out_specs=[vmem_spec(), any_spec()],
        out_shape=[pltpu.VMEM((slots, feats - first), F32), pltpu.HBM((sum(counts), feats), BF16)],
        scratch_shapes=[pltpu.SemaphoreType.DMA((len(scaled),))],
        compiler_params=params(6),
        cost_estimate=declared(),
        name="expert_out_rest",
    )(hidden, weight, *scaled)


def column(row):
    return jnp.broadcast_to(row, (8, row.shape[1])).T[:, :1]


def gate_of(chunk_ref, me, half, lower):
    by = chunk_ref[chunk_ref.shape[0] - 16 :, :].astype(F32)
    row = lax.broadcasted_iota(jnp.int32, by.shape, 0)
    gate = jnp.sum(jnp.where(row == me, by, 0.0), axis=0, keepdims=True)
    return column(gate)[lower * half : (lower + 1) * half]


def add_up(chunk_ref, eo_refs, at, half):
    total = jnp.zeros((half, LANES), F32)
    j = 0
    for ref in eo_refs:
        for k in range(ref.shape[1] // LANES):
            value = chunk_ref[j * half : (j + 1) * half, :].astype(F32)
            total = total + value * ref[at : at + half, k * LANES : (k + 1) * LANES]
            j += 1
    return jnp.sum(total, axis=1, keepdims=True)


def put_scaled(chunk_ref, out_ref, at, gate, half):
    for j in range(out_ref.shape[1] // LANES):
        value = chunk_ref[j * half : (j + 1) * half, :].astype(F32)
        out_ref[at : at + half, j * LANES : (j + 1) * LANES] = (value * gate).astype(BF16)


def scaled_rows(info, chunks, lowers, half, flops):
    cols = (chunks[0].shape[0] - 16) // half
    count = len(chunks)

    def body(info_ref, *refs):
        out_ref = refs[count]
        for i, ref in enumerate(refs[:count]):
            put_scaled(ref, out_ref, i * half, gate_of(ref, info_ref[1], half, lowers[i]), half)

    return pl.pallas_call(
        body,
        in_specs=[smem_spec()] + [vmem_spec()] * count,
        out_specs=vmem_spec(),
        out_shape=pltpu.VMEM((count * half, cols * LANES), BF16),
        compiler_params=params(3),
        cost_estimate=declared(flops),
        name="scaled_rows",
    )(info, *chunks)


def absorb(info, chunks, expert_out, tokens, steps):
    half = tokens // 2
    experts = expert_out[0].shape[0] // tokens
    count = len(chunks) // 2

    def body(info_ref, *refs):
        chunk_refs, eo_refs = refs[: 2 * count], refs[2 * count : 2 * count + 2]
        sums_ref, last_ref, own_ref = refs[2 * count + 2 :]
        me = info_ref[1]
        lanes = []
        for i in range(count):
            at = i * tokens
            sums = [add_up(chunk_refs[2 * i + c], eo_refs, at + c * half, half) for c in range(2)]
            lanes.append(jnp.concatenate(sums, axis=0))
        lanes += [jnp.zeros((tokens, 1), F32)] * (experts - count)
        by_step = jnp.concatenate(lanes, axis=1).T
        row = lax.broadcasted_iota(jnp.int32, (experts, tokens), 0)
        total = jnp.zeros((experts, tokens), F32)
        for i, step in enumerate(steps[:count]):
            total = jnp.where(row == source_of(me, step, experts), by_step[i : i + 1], total)
        sums_ref[...] = total
        last_ref[...] = (row == source_of(me, steps[-1], experts)).astype(F32)
        own_ref[...] = (lax.broadcasted_iota(jnp.int32, own_ref.shape, 0) == me).astype(F32)

    return pl.pallas_call(
        body,
        in_specs=[smem_spec()] + [vmem_spec()] * (2 * count + 2),
        out_specs=[vmem_spec()] * 3,
        out_shape=[
            pltpu.VMEM((experts, tokens), F32),
            pltpu.VMEM((experts, tokens), F32),
            pltpu.VMEM((16, LANES), F32),
        ],
        compiler_params=params(4),
        cost_estimate=declared(),
        name="absorb",
    )(info, *chunks, *expert_out)


def absorb_last(chunks, expert_out, sums, mask, groups):
    experts, tokens = sums.shape
    half = tokens // 2
    first = expert_out[0].shape[0] - tokens

    def body(top_ref, bottom_ref, eo_ref, rest_ref, sums_ref, mask_ref, out_ref):
        parts = [add_up(ref, (eo_ref, rest_ref), first + c * half, half) for c, ref in enumerate((top_ref, bottom_ref))]
        own = jnp.broadcast_to(jnp.concatenate(parts, axis=0), (tokens, experts)).T
        value = jnp.where(mask_ref[...] > 0.0, own, sums_ref[...])
        out_ref[...] = jnp.broadcast_to(value[:, None, :], out_ref.shape)

    return pl.pallas_call(
        body,
        in_specs=[vmem_spec()] * 6,
        out_specs=vmem_spec(),
        out_shape=jax.ShapeDtypeStruct((experts, groups, tokens), F32),
        compiler_params=params(2),
        cost_estimate=declared(),
        name="absorb_last",
    )(*chunks, *expert_out, sums, mask)


def weight_grad(own, early, early_places, late, late_places, chunks, chunk_places, hidden_t):
    units, slots = hidden_t.shape
    feats = late[0].shape[1]
    half = late[0].shape[0] // len(late_places[0])
    blocks = 4
    rows = units // blocks

    def body(own_ref, early_ref, *refs):
        late_refs, refs = refs[: len(late)], refs[len(late) :]
        chunk_refs, refs = refs[: len(chunks)], refs[len(chunks) :]
        ht_ref, out_ref, rows_scr, held, in_sems, out_sems = refs
        copies = [
            pltpu.make_async_copy(
                early_ref.at[pl.ds(i * half, half)], rows_scr.at[pl.ds(place, half)], in_sems.at[i]
            )
            for i, place in enumerate(early_places)
        ]
        for copy in copies:
            copy.start()
        for ref, at in zip(late_refs, late_places):
            for i, place in enumerate(at):
                rows_scr[place : place + half, :] = ref[i * half : (i + 1) * half, :]
        for ref, (place, lower) in zip(chunk_refs, chunk_places):
            by = ref[ref.shape[0] - 16 :, :].astype(F32)
            gate = column(jnp.sum(by * own_ref[...], axis=0, keepdims=True))[lower * half : (lower + 1) * half]
            put_scaled(ref, rows_scr, place, gate, half)
        for copy in copies:
            copy.wait()
        copies = []
        for i in range(blocks):
            here = pl.ds(i * rows, rows)
            held[here, :] = jnp.dot(ht_ref[here, :], rows_scr[...], preferred_element_type=F32).astype(BF16)
            copy = pltpu.make_async_copy(held.at[here], out_ref.at[here], out_sems.at[i])
            copy.start()
            copies.append(copy)
        for copy in copies:
            copy.wait()

    return pl.pallas_call(
        body,
        in_specs=[vmem_spec(), any_spec()] + [vmem_spec()] * (1 + len(late) + len(chunks)),
        out_specs=any_spec(),
        out_shape=jax.ShapeDtypeStruct((units, feats), BF16),
        scratch_shapes=[
            pltpu.VMEM((slots, feats), BF16),
            pltpu.VMEM((units, feats), BF16),
            pltpu.SemaphoreType.DMA((len(early_places),)),
            pltpu.SemaphoreType.DMA((blocks,)),
        ],
        compiler_params=params(12),
        cost_estimate=declared(),
        name="weight_grad",
    )(own, in_hbm(early), *late, *chunks, hidden_t)


def pick(returned, routes_t):
    topk, tokens = routes_t.shape
    experts, groups, _ = returned.shape

    def body(back_ref, routes_ref, out_ref):
        routes = routes_ref[...]
        total = jnp.zeros((topk, tokens), F32)
        for e in range(experts):
            value = jnp.sum(back_ref[e], axis=0, keepdims=True)
            total = jnp.where(routes == e, jnp.broadcast_to(value, total.shape), total)
        out_ref[...] = total

    return pl.pallas_call(
        body,
        in_specs=[vmem_spec(), vmem_spec()],
        out_specs=vmem_spec(),
        out_shape=jax.ShapeDtypeStruct((topk, tokens), F32),
        compiler_params=params(2),
        name="pick_gate_grad",
    )(returned, routes_t)


def dense(out_grad, gate_weights, routes, gate_pre, up_pre, down_weight):
    tokens, topk = routes.shape
    experts, groups = lax.axis_size("ep"), lax.axis_size("et")
    weight = down_weight[0]
    barrier = lax.optimization_barrier

    ring = ring_of(experts)
    forth = [(ring[i], ring[(i + 1) % experts]) for i in range(experts)]
    back = [(b, a) for a, b in forth]
    far = experts // 2
    steps = [0] + [s for k in range(1, far) for s in (-k, k)] + [far]
    info = jnp.stack([lax.axis_index("et").astype(jnp.int32), lax.axis_index("ep").astype(jnp.int32)])
    out_grad, info = barrier((out_grad, info))

    top, bottom = chunks_of(out_grad, gate_weights.T, routes.T)
    hidden, weight = hidden_of(gate_pre[0], up_pre[0], weight)
    chips, cores = [(i, i ^ 2) for i in range(groups)], [(i, i ^ 1) for i in range(groups)]
    half = tokens // 2

    def hop(c):
        up[c] = lax.ppermute(up[c], "ep", forth)
        down[c] = lax.ppermute(down[c], "ep", back)

    def scale(chunks, lowers, flops=0):
        return scaled_rows(info, chunks, lowers, half, flops)

    up, down = [top, bottom], [bottom, top]
    hop(0)
    hop(1)
    over = lax.ppermute(hidden, "et", chips)
    beside, across = lax.ppermute(hidden, "et", cores), lax.ppermute(over, "et", cores)
    up[0], down[0] = barrier((up[0], down[0]))
    first = [up[0], up[1], down[1], down[0]]
    hop(0)
    hop(1)
    second = [up[0], up[1], down[1], down[0]]
    scaled_a = scale([top, bottom] + first, [0, 1] * 3, 4e9)
    up[0], down[0], scaled_a = barrier((up[0], down[0], scaled_a))
    hop(0)
    scaled_b = scale(second, [0, 1] * 2, 8e9)
    up[1], down[1], scaled_b = barrier((up[1], down[1], scaled_b))
    hop(1)
    cut = weight.shape[1] // 256 * 3 // 7 * 256
    hidden, hidden_t, start = assemble(info, [hidden, beside, over, across], weight, tokens, steps, cut)
    up[0], down[0], hidden_t = barrier((up[0], down[0], hidden_t))
    third = [up[0], up[1], down[1], down[0]]
    scaled_c = scale([up[0], down[0]], [0, 1], 12e9)
    up[0], down[0], scaled_c = barrier((up[0], down[0], scaled_c))

    hop(0)
    rest, early = expert_out_rest(hidden, weight, [scaled_a, scaled_b], cut)
    expert_out = [start, rest]
    third, early = barrier((third, early))
    sums, mask, own = absorb(info, [top, bottom] + first + second + third, expert_out, tokens, steps)
    outgoing = absorb_last([up[0], down[0]], expert_out, sums, mask, groups)
    returned = lax.all_to_all(
        outgoing.reshape(experts * groups, tokens), ("ep", "et"), split_axis=0, concat_axis=0, tiled=True
    )
    chunks = [third[1], third[2], up[0], down[0]]
    chunk_places = [(11 * half, 1), (12 * half, 0), (14 * half, 0), (15 * half, 1)]
    grad = weight_grad(
        own, early, [i * half for i in range(10)], [scaled_c], [[10 * half, 13 * half]], chunks, chunk_places, hidden_t
    )
    d_gate = pick(returned.reshape(experts, groups, tokens), routes.T).T
    return grad[None], d_gate


def routed(out_grad, gate_weights, routes, gate_pre, up_pre, down_weight):
    tok_rows, topk = routes.shape
    experts = lax.axis_size("ep")
    slot_total = gate_pre.shape[1]
    capacity = slot_total // experts
    flat_route = routes.reshape(-1)
    pair_count = tok_rows * topk
    onehot = (flat_route[:, None] == jnp.arange(experts, dtype=jnp.int32)[None, :]).astype(
        jnp.int32
    )
    ranks = jnp.sum(jnp.cumsum(onehot, axis=0) * onehot, axis=1) - 1
    slot_of = flat_route * capacity + ranks
    pair_ids = jnp.arange(pair_count, dtype=jnp.int32)
    slot_pair = jnp.zeros((experts * capacity,), jnp.int32).at[slot_of].set(pair_ids)
    filled = jnp.zeros((experts * capacity,), jnp.bool_).at[slot_of].set(True)
    send_rows = jnp.where(filled[:, None], out_grad[slot_pair // topk], 0.0)
    send_rows = send_rows.reshape(experts, capacity, out_grad.shape[1])
    send_gates = jnp.where(filled, gate_weights.reshape(-1)[slot_pair], 0.0)
    send_gates = send_gates.reshape(experts, capacity)
    rows_in, gates_in = (
        lax.all_to_all(send_rows, "ep", split_axis=0, concat_axis=0, tiled=True),
        lax.all_to_all(send_gates, "ep", split_axis=0, concat_axis=0, tiled=True),
    )
    rows_in = rows_in.reshape(slot_total, out_grad.shape[1])
    gates_in = gates_in.reshape(slot_total)
    weight = down_weight[0]
    hidden_part = (
        jax.nn.silu(gate_pre[0].astype(jnp.float32)) * up_pre[0].astype(jnp.float32)
    ).astype(jnp.bfloat16)
    scaled = (gates_in.astype(jnp.float32)[:, None] * rows_in.astype(jnp.float32)).astype(
        jnp.bfloat16
    )
    piece = lax.all_gather(hidden_part, "et", axis=1, tiled=True)
    expert_out = jnp.dot(piece, weight, preferred_element_type=jnp.float32)
    grad_weight = lax.dot_general(
        piece, scaled, (((0,), (0,)), ((), ())), preferred_element_type=jnp.float32
    )
    partial_grad = jnp.sum(rows_in.astype(jnp.float32) * expert_out, axis=1)
    slot_grad = lax.psum(partial_grad, "et")
    returned = lax.all_to_all(
        slot_grad.reshape(experts, capacity), "ep", split_axis=0, concat_axis=0, tiled=True
    )
    d_gate = returned.reshape(-1)[slot_of].reshape(tok_rows, topk)
    return (grad_weight.astype(jnp.bfloat16)[None], d_gate)


def solution(mesh):
    sizes = dict(mesh.shape)

    def local(out_grad, gate_weights, routes, gate_pre, up_pre, down_weight):
        tokens, topk = routes.shape
        whole = topk == sizes["ep"] and gate_pre.shape[1] == topk * tokens
        if whole and sizes["ep"] == 8 and sizes["et"] == 4:
            return dense(out_grad, gate_weights, routes, gate_pre, up_pre, down_weight)
        return routed(out_grad, gate_weights, routes, gate_pre, up_pre, down_weight)

    in_specs = (
        P("ep", "et"),
        P("ep", None),
        P("ep", None),
        P("ep", None, "et"),
        P("ep", None, "et"),
        P("ep", None, "et"),
    )
    out_specs = (P("ep", None, "et"), P("ep", None))
    return jax.shard_map(local, mesh=mesh, in_specs=in_specs, out_specs=out_specs, check_vma=False)
```
